32 devices in a mesh: comp: 2 (over core), tile: 16 (over z, y, x).
Axes of the slice: x: 2, y: 2, z: 4, core: 2. Of those that a mesh axis runs over, the one named last changes fastest.
Arguments:
- state: float32 [2, 256, 256], P('comp', 'tile'), may hold values from -6 to 6
- coeff: float32 [2, 256, 256], P('comp', 'tile'), may hold values from 0.3 to 3
- vertical: int32 [256, 256], P('tile'), may hold values from 0 to 5
- send_cell: int32 [256, 4096], P(('comp', 'tile')), may hold values from 0 to 4095, as said below
- incoming_marine_slot: int32 [256, 4096], P(('comp', 'tile')), may hold values from 0 to 4095, as said below
- remap_weight: float32 [256, 4096], P(('comp', 'tile')), as said below
Outputs:
- exchanged_pair: float32 [2, 256, 256], P('comp', 'tile')
The draws below stay inside these ranges and needn't reach their ends.
Inputs may be any that keep to these rules, and one draw needn't show every extreme that they name: `send_cell`: rows of ocean partitions (index 128 and above) are 0. Rows d = 3 and d = 5 of every atmosphere partition are full; rows 0 and 1, 2 and 4, 6 and 7 come in pairs whose live slots fill one row together. Live slots lead each row; dead slots hold cell 0. Every atmosphere cell is named by exactly five live slots of its partition. `incoming_marine_slot`: rows of atmosphere partitions are 0. Row (16 + t) * 8 + d names the ocean cell of the slot that send_cell row ((t - d + 4) mod 16) * 8 + d names; dead slots hold 0. `remap_weight`: live slots have weights of at least 0.25; dead slots and rows of ocean partitions 0.
All inputs are finite; a program needn't handle non-finite values.
Results may differ from the reference program's by a relative error of at most 0.00002.
Values sent between devices are 32-bit elements; how exact they have to be, the bound alone decides.
No kernel may reach another device: no remote copies, remote signals or barrier semaphores. Data moves between devices by JAX's collectives and lax.ppermute only.
A program may use at most 64 MiB of HBM per device.

```python
import math
import jax
import jax.numpy as jnp

SIDE_LENGTH = 256
SPAN = 8
SWEEPS = 20
DOMAIN_PIECES = 16
PEERS = 32
MESH_LINES = 256
BLOCK_POINTS = 4096


def intersection_tables(key):
    base = jax.random.fold_in(key, 4111)
    k_cut, k_cell, k_shift, k_weight, k_perm = jax.random.split(base, 5)
    cuts = jax.random.randint(k_cut, (DOMAIN_PIECES, 3), 0, BLOCK_POINTS // 2 + 1)
    full = jnp.full((DOMAIN_PIECES, 1), BLOCK_POINTS, jnp.int32)
    counts = jnp.concatenate([BLOCK_POINTS - cuts[:, 0:1], cuts[:, 0:1], BLOCK_POINTS - cuts[:, 1:2], full, cuts[:, 1:2], full, BLOCK_POINTS - cuts[:, 2:3], cuts[:, 2:3]], axis=1)
    starts = jnp.cumsum(counts, axis=1) - counts
    slot = jnp.arange(BLOCK_POINTS, dtype=jnp.int32)
    live = slot[None, None, :] < counts[:, :, None]
    order_ids = jnp.clip((starts[:, :, None] + slot[None, None, :]) // 5, 0, BLOCK_POINTS - 1).astype(jnp.int32)
    perm_keys = jax.random.split(k_perm, DOMAIN_PIECES)
    shuffles = jax.vmap(lambda one_key: jax.random.permutation(one_key, BLOCK_POINTS))(perm_keys).astype(jnp.int32)
    permuted = jnp.take_along_axis(shuffles, order_ids.reshape(DOMAIN_PIECES, SPAN * BLOCK_POINTS), axis=1).reshape(DOMAIN_PIECES, SPAN, BLOCK_POINTS)
    atm_cell = jnp.where(live, permuted, 0)
    shift = jax.random.randint(k_shift, (DOMAIN_PIECES, 1), 0, BLOCK_POINTS)
    random_cells = jax.random.randint(k_cell, (DOMAIN_PIECES, SPAN, BLOCK_POINTS), 0, BLOCK_POINTS)
    first_cells = (slot[None, :] + shift) % BLOCK_POINTS
    ocean_cell = jnp.where(live, random_cells.at[:, 0, :].set(first_cells), 0)
    weight = jnp.where(live, jax.random.uniform(k_weight, (DOMAIN_PIECES, SPAN, BLOCK_POINTS), jnp.float32, 0.25, 1.0), 0.0)
    tile_ids = jnp.arange(DOMAIN_PIECES, dtype=jnp.int32)[:, None]
    offset_ids = jnp.arange(SPAN, dtype=jnp.int32)[None, :]
    source = (tile_ids - offset_ids + SPAN // 2) % DOMAIN_PIECES
    ocean_rows = ocean_cell[source, offset_ids]
    zero_int = jnp.zeros((DOMAIN_PIECES, SPAN, BLOCK_POINTS), jnp.int32)
    sends = jnp.concatenate([atm_cell, zero_int], axis=0)
    arrived_numbers = jnp.concatenate([zero_int, ocean_rows], axis=0)
    weights = jnp.concatenate([weight, jnp.zeros((DOMAIN_PIECES, SPAN, BLOCK_POINTS), jnp.float32)], axis=0)
    return (sends.reshape(PEERS * SPAN, BLOCK_POINTS), arrived_numbers.reshape(PEERS * SPAN, BLOCK_POINTS), weights.reshape(PEERS * SPAN, BLOCK_POINTS))


def draw_send_cell(key, part):
    return intersection_tables(key)[0]


def draw_incoming_marine_slot(key, part):
    return intersection_tables(key)[1]


def draw_remap_weight(key, part):
    return intersection_tables(key)[2]


def touch_ends(result, stream_key, least, top_value):
    longest = result.shape.index(max(result.shape))
    spots = []
    for shift in (0, 1):
        where = [jax.random.randint(jax.random.fold_in(stream_key, axis), (), 0, length) for axis, length in enumerate(result.shape)]
        where[longest] = (where[longest] + shift) % result.shape[longest]
        spots.append(tuple(where))
    return result.at[spots[0]].set(least).at[spots[1]].set(top_value)


def steps_of(own_key, shape, shards, least, largest):
    def one(axis_at, shards_of):
        steps = jax.random.uniform(jax.random.fold_in(jax.random.fold_in(own_key, 6), axis_at), (shards_of,), jnp.float32, least / len(shards), largest / len(shards))
        return jnp.repeat(jnp.exp(steps), shape[axis_at] // shards_of).reshape((-1,) + (1,) * (len(shape) - axis_at - 1))

    gain = one(*shards[0])
    for cut in shards[1:]:
        gain = gain * one(*cut)
    return gain


def centred(key, shape, width, limit, cuts=(), kind=jnp.bfloat16):
    loudness = steps_of(key, shape, cuts, -0.22, 0.18) if cuts else 1.0
    values = jax.random.normal(key, shape, jnp.float32) * width * loudness
    return jnp.minimum(jnp.maximum(values, -limit), limit).astype(kind)


def setup_inputs(seed: int = 0) -> dict:
    keys = jax.random.split(jax.random.key(seed), 7)
    state = centred(keys[0], (2, MESH_LINES, SIDE_LENGTH), 1.0, 6.0, ((0, 2), (1, 16)), jnp.float32)
    coeff = jnp.clip(jnp.exp(math.log(3.0) - 2.3025851 * jax.random.uniform(keys[1], (2, MESH_LINES, SIDE_LENGTH), jnp.float32) ** steps_of(keys[1], (2, MESH_LINES, SIDE_LENGTH), ((0, 2), (1, 16)), -0.2, 0.2)), 0.3, 3.0)
    vertical = touch_ends(jax.random.randint(keys[2], (MESH_LINES, SIDE_LENGTH), 0, 6), jax.random.fold_in(keys[2], 1), 0, 5).astype(jnp.int32)
    send_cell = draw_send_cell(jax.random.fold_in(keys[6], 71), 0)
    incoming_marine_slot = draw_incoming_marine_slot(jax.random.fold_in(keys[6], 71), 0)
    remap_weight = draw_remap_weight(jax.random.fold_in(keys[6], 71), 0)
    return dict(state=state, coeff=coeff, vertical=vertical, send_cell=send_cell, incoming_marine_slot=incoming_marine_slot, remap_weight=remap_weight)


def reference(state, coeff, vertical, send_cell, incoming_marine_slot, remap_weight):
    air = state[0]
    marine_solution = state[1]
    near = jnp.roll(air, 1, 0) + jnp.roll(air, -1, 0) + jnp.roll(air, 1, 1) + jnp.roll(air, -1, 1)
    air_flux = (coeff[0] * (air + 0.2 * (near - 4.0 * air))).reshape(DOMAIN_PIECES, BLOCK_POINTS)
    sends = send_cell.reshape(PEERS, SPAN, BLOCK_POINTS)[:DOMAIN_PIECES]
    weights = remap_weight.reshape(PEERS, SPAN, BLOCK_POINTS)[:DOMAIN_PIECES]
    ocean_rows = incoming_marine_slot.reshape(PEERS, SPAN, BLOCK_POINTS)[DOMAIN_PIECES:]
    source_ids = jnp.arange(DOMAIN_PIECES, dtype=jnp.int32)
    offset_ids = jnp.arange(SPAN, dtype=jnp.int32)
    target_model = ((source_ids[:, None] + offset_ids[None, :] - SPAN // 2) % DOMAIN_PIECES).astype(jnp.int32)
    arrived_numbers = ocean_rows[target_model, offset_ids[None, :]]
    picked = air_flux[source_ids[:, None, None], sends]
    ocean_flat = (target_model[:, :, None] * BLOCK_POINTS + arrived_numbers).astype(jnp.int32)
    ocean_source = jnp.zeros((DOMAIN_PIECES * BLOCK_POINTS,), jnp.float32).at[ocean_flat.reshape(-1)].add((weights * picked).reshape(-1))
    source_mesh = ocean_source.reshape(MESH_LINES, SIDE_LENGTH)
    rhs = source_mesh + marine_solution
    diag = coeff[1] + 3.0
    row_ids = jnp.arange(MESH_LINES, dtype=jnp.int32)[:, None]
    col_ids = jnp.arange(SIDE_LENGTH, dtype=jnp.int32)[None, :]
    up_down = vertical // 3
    sideways = vertical % 3 - 1
    index = (((row_ids - 1 + 2 * up_down) % MESH_LINES) * SIDE_LENGTH + (col_ids + sideways) % SIDE_LENGTH).astype(jnp.int32)
    elevation_trace = jnp.zeros((MESH_LINES, SIDE_LENGTH), jnp.float32)
    for sweep in range(SWEEPS):
        beside_all = jnp.roll(elevation_trace, 1, 1) + jnp.roll(elevation_trace, -1, 1) + jnp.take(elevation_trace.reshape(-1), index)
        elevation_trace = (rhs + beside_all) / diag
    fresh_skin_heat = (marine_solution + 0.5 * elevation_trace - 0.25 * source_mesh).reshape(DOMAIN_PIECES, BLOCK_POINTS)
    number_listing = fresh_skin_heat[target_model[:, :, None], arrived_numbers]
    air_flat = (source_ids[:, None, None] * BLOCK_POINTS + sends).astype(jnp.int32).reshape(-1)
    share_accumulated = jnp.zeros((DOMAIN_PIECES * BLOCK_POINTS,), jnp.float32).at[air_flat].add(weights.reshape(-1))
    overall_quantity = jnp.zeros((DOMAIN_PIECES * BLOCK_POINTS,), jnp.float32).at[air_flat].add((weights * number_listing).reshape(-1))
    measured_skin_heat = (overall_quantity / share_accumulated).reshape(MESH_LINES, SIDE_LENGTH)
    return jnp.stack([measured_skin_heat, elevation_trace])
```

```python
import jax
import jax.experimental.pallas as pl
import jax.experimental.pallas.tpu as pltpu
import jax.numpy as jnp
from jax import lax
from jax.sharding import PartitionSpec as P

SPAN = 8
SWEEPS = 20
MIDDLE = SPAN // 2
F32 = jnp.float32
BF16 = jnp.bfloat16
I32 = jnp.int32
CONTRACT_LANES = (((1,), (1,)), ((), ()))
GRID = ("comp", "tile")


def call(kernel, shapes, *operands, scratch=()):
    out = [jax.ShapeDtypeStruct(shape, F32) for shape in shapes]
    return pl.pallas_call(
        kernel,
        out_shape=out,
        in_specs=[pl.BlockSpec(memory_space=pltpu.VMEM)] * len(operands),
        out_specs=[pl.BlockSpec(memory_space=pltpu.VMEM)] * len(out),
        scratch_shapes=scratch,
        compiler_params=pltpu.CompilerParams(vmem_limit_bytes=32 * 1024 * 1024),
    )(*operands)


def on_each_component(atmosphere, ocean):
    comp = lax.axis_index("comp")
    pl.when(comp == 0)(atmosphere)
    pl.when(comp != 0)(ocean)


def fold_row(source, row, target, first):
    width = target.shape[1]
    for j in range(source.shape[1] // width):
        piece = source[row : row + 1, j * width : (j + 1) * width]
        target[first + j : first + j + 1, :] = piece.astype(F32)


def gather_cells(table, index):
    rows, width = index.shape
    tiles = [(r, h) for r in range(0, rows, 8) for h in range(0, width, 128)]
    pieces = [index[r : r + 8, h : h + 128] for r, h in tiles]
    high = [lax.shift_right_logical(p, 7) for p in pieces]
    low = [p & 127 for p in pieces]
    found = [jnp.zeros((8, 128), F32) for _ in tiles]
    for i in range(rows * width // 128):
        r, h = divmod(i * 128, width)
        line = jnp.broadcast_to(table[r : r + 1, h : h + 128], (8, 128))
        for k in range(len(tiles)):
            picked = jnp.take_along_axis(line, low[k], axis=1, mode="promise_in_bounds")
            found[k] = jnp.where(high[k] == i, picked, found[k])
    across = width // 128
    return jnp.concatenate(
        [jnp.concatenate(found[k : k + across], 1) for k in range(0, len(found), across)], 0
    )


def scatter_add(total, values, index):
    rows, width = index.shape
    place = lax.broadcasted_iota(I32, (64, width), 0)
    for r in range(rows):
        cell = index[r : r + 1, :]
        value = values[r : r + 1, :]
        head = value.astype(BF16).astype(F32)
        tail = value - head
        row_here = place == lax.shift_right_logical(cell, 6)
        column_here = place == (cell & 63)
        spread = jnp.concatenate(
            [
                jnp.where(row_here, head, 0.0).astype(BF16),
                jnp.where(row_here, tail, 0.0).astype(BF16),
            ],
            0,
        )
        chosen = jnp.where(column_here, 1.0, 0.0).astype(BF16)
        total = total + lax.dot_general(
            spread, chosen, CONTRACT_LANES, preferred_element_type=F32
        )
    return total


def as_rows(total):
    both = total[:64] + total[64:]
    cells = both.reshape(16, 4, 64)
    return jnp.concatenate([cells[:, q, :] for q in range(4)], 1)


def pack_kernel(
    cells, weights, slots, state, coeff, cells_sw, weights_sw, slots_sw, state_sw, coeff_sw, vertical,
    m0, m1, m2, m3, edge, n0, n1, n2, n3,
):
    forward = (m0, m1, m2, m3)
    static = (n0, n1, n2, n3)

    def fill(cells, weights, slots, state0, coeff0, state1, coeff1, rows, rows_back):
        for j in range(4):
            fold_row(cells, rows[j], forward[j], 0)
            fold_row(weights, rows[j], forward[j], 16)
            forward[j][32:48, :] = state0[0]
            forward[j][48:64, :] = coeff0[0]
            fold_row(slots, rows_back[j], static[j], 0)
            static[j][16:32, :] = coeff1[0]
            static[j][32:48, :] = vertical[...].astype(F32)
            static[j][48:64, :] = state1[0]
        edge[...] = state0[0, 0:8, :]

    on_each_component(
        lambda: fill(cells, weights, slots_sw, state, coeff, state_sw, coeff_sw, (3, 2, 1, 0), (5, 6, 7, 4)),
        lambda: fill(cells_sw, weights_sw, slots, state_sw, coeff_sw, state, coeff, (4, 5, 6, 7), (3, 2, 1, 0)),
    )


def local_kernel(cells, weights, slots, cells_sw, weights_sw, slots_sw, near_slots, far_cells, far_weights, inverse):
    def fill(cells, weights, slots, rows, rows_back):
        for j in range(4):
            fold_row(slots, rows[j], near_slots, 16 * j)
            fold_row(cells, rows_back[j], far_cells, 16 * j)
            fold_row(weights, rows_back[j], far_weights, 16 * j)

    def atmosphere():
        fill(cells, weights, slots_sw, (3, 2, 1, 0), (4, 5, 6, 7))
        total = jnp.zeros((128, 64), F32)
        for d in range(SPAN):
            for j in range(0, cells.shape[1], 256):
                total = scatter_add(total, weights[d : d + 1, j : j + 256], cells[d : d + 1, j : j + 256])
        inverse[...] = 1.0 / as_rows(total)

    def ocean():
        fill(cells_sw, weights_sw, slots, (4, 5, 6, 7), (0, 1, 2, 3))
        inverse[...] = jnp.ones_like(inverse)

    on_each_component(atmosphere, ocean)


def flux_kernel(own, r0, r1, r2, r3, edge, near_slots, partial):
    atmosphere = lax.axis_index("comp") == 0
    first = jnp.where(atmosphere, r0[...], own[...])
    blocks = (first, r1[...], r2[...], r3[...])
    air = [b[32:48] for b in blocks]
    top = [a[0:1] for a in air]
    bottom = [a[15:16] for a in air]
    beyond = edge[0:1]
    total = jnp.zeros((128, 64), F32)
    for j in range(4):
        if j == 0:
            before = jnp.where(atmosphere, own[47:48], bottom[1])
        elif j < 3:
            before = jnp.where(atmosphere, bottom[j - 1], bottom[j + 1])
        else:
            before = jnp.where(atmosphere, bottom[2], r0[47:48])
        if j == 0:
            after = jnp.where(atmosphere, top[1], beyond)
        elif j < 3:
            after = jnp.where(atmosphere, top[j + 1], top[j - 1])
        else:
            after = jnp.where(atmosphere, beyond, top[2])
        s = air[j]
        near = jnp.concatenate([before, s[:-1]], 0) + jnp.concatenate([s[1:], after], 0)
        near = near + pltpu.roll(s, 1, 1) + pltpu.roll(s, s.shape[1] - 1, 1)
        flux = blocks[j][48:64] * (s + 0.2 * (near - 4.0 * s))
        picked = gather_cells(flux, blocks[j][0:16].astype(I32))
        slot = near_slots[16 * j : 16 * j + 16].astype(I32)
        total = scatter_add(total, blocks[j][16:32] * picked, slot)
    partial[...] = as_rows(total)


def source_kernel(partial, partial_sw, own, rhs, back, low, high):
    total = partial[...] + partial_sw[...] + own[48:64]
    rhs[...] = total
    back[0:16, :] = total
    back[16:48, :] = own[16:48]
    for k, rows in enumerate((total, own[16:32], own[32:48])):
        low[8 * k : 8 * k + 8, :] = rows[8:16]
        high[8 * k : 8 * k + 8, :] = rows[0:8]


def trace_kernel(
    rhs_own, p0, p1, p2, p3, p4, p5, p6, n_own, n0, n1, n2, n3, far_cells, far_weights,
    send, keep, rhs, inv, code, eta, left, right,
):
    rows = rhs.shape[0]
    pad = 8
    inner = rows

    def place(parts):
        at = 0
        for r, c, v in parts:
            size = r.shape[0]
            rhs[at : at + size, :] = r[...]
            inv[at : at + size, :] = 1.0 / (c[...] + 3.0)
            code[at : at + size, :] = v[...]
            at += size

    lo = (p5.at[0:8], p5.at[8:16], p5.at[16:24])
    hi = (p6.at[0:8], p6.at[8:16], p6.at[16:24])
    back = (p4.at[0:16], p4.at[16:32], p4.at[32:48])
    own = (rhs_own, n_own.at[16:32], n_own.at[32:48])
    near = [(p, n.at[16:32], n.at[32:48]) for p, n in zip((p0, p1, p2, p3), (n0, n1, n2, n3))]
    on_each_component(
        lambda: place([lo, back, own, *near, hi]),
        lambda: place([lo, back, *near[::-1], own, hi]),
    )
    zero = jnp.zeros((inner + 2 * pad, rhs.shape[1]), F32)
    eta[...] = zero
    left[...] = zero
    right[...] = zero
    width = rhs.shape[1]

    def sweep(step, carry):
        for b in range(0, inner, 16):
            here = eta[pad + b : pad + b + 16, :]
            left[pad + b : pad + b + 16, :] = pltpu.roll(here, 1, 1)
            right[pad + b : pad + b + 16, :] = pltpu.roll(here, width - 1, 1)
        fresh = []
        for b in range(0, inner, 16):
            v = code[b : b + 16, :]
            down = v >= 3.0
            side = jnp.where(down, v - 3.0, v)
            third = []
            for ref in (left, eta, right):
                above = ref[pad + b - 1 : pad + b + 15, :]
                below = ref[pad + b + 1 : pad + b + 17, :]
                third.append(jnp.where(down, below, above))
            picked = jnp.where(side == 0.0, third[0], jnp.where(side == 1.0, third[1], third[2]))
            beside = left[pad + b : pad + b + 16, :] + right[pad + b : pad + b + 16, :] + picked
            fresh.append((rhs[b : b + 16, :] + beside) * inv[b : b + 16, :])
        for k, b in enumerate(range(0, inner, 16)):
            eta[pad + b : pad + b + 16, :] = fresh[k]
        return carry

    lax.fori_loop(0, SWEEPS, sweep, 0)

    atmosphere = lax.axis_index("comp") == 0
    surface = [jnp.where(atmosphere, n_own[48:64], n3[48:64])]
    slots = [jnp.where(atmosphere, n_own[0:16], n3[0:16])]
    for i, (up, down) in enumerate(((n0, n2), (n1, n1), (n2, n0))):
        surface.append(jnp.where(atmosphere, up[48:64], down[48:64]))
        slots.append(jnp.where(atmosphere, up[0:16], down[0:16]))
    total = jnp.zeros((128, 64), F32)
    for i in range(4):
        at = 24 + 16 * i
        sst = 1.25 * surface[i] + 0.5 * eta[pad + at : pad + at + 16, :] - 0.25 * rhs[at : at + 16, :]
        picked = gather_cells(sst, slots[i].astype(I32))
        cell = far_cells[16 * i : 16 * i + 16].astype(I32)
        total = scatter_add(total, far_weights[16 * i : 16 * i + 16] * picked, cell)
    part = as_rows(total)
    send[...] = jnp.where(atmosphere, eta[pad + 24 : pad + 40, :], part)
    keep[...] = jnp.where(atmosphere, part, 0.0)


def shards(state, coeff, vertical, send_cell, incoming_marine_slot, remap_weight):
    tiles = lax.axis_size("tile")
    block = state.shape[1:]

    def swap(x):
        return lax.ppermute(x, "comp", [(0, 1), (1, 0)])

    def move(x, atmosphere_from, ocean_from):
        pairs = [((t + atmosphere_from) % tiles, t) for t in range(tiles)]
        pairs += [(tiles + (t + ocean_from) % tiles, tiles + t) for t in range(tiles)]
        return lax.ppermute(x, GRID, pairs)

    cells_sw, weights_sw, slots_sw = swap(send_cell), swap(remap_weight), swap(incoming_marine_slot)
    state_sw, coeff_sw = swap(state), swap(coeff)
    lines, width = block
    packed = call(
        pack_kernel,
        [(4 * lines, width)] * 4 + [(8, width)] + [(4 * lines, width)] * 4,
        send_cell, remap_weight, incoming_marine_slot, state, coeff,
        cells_sw, weights_sw, slots_sw, state_sw, coeff_sw, vertical,
    )
    forward, edge, static = packed[:4], packed[4], packed[5:]
    edge_in = move(edge, 5, 1)
    forward_in = [move(forward[j], 1 + j, -j if j else -4) for j in (3, 2, 1, 0)][::-1]
    static_in = [move(static[j], 1 + j, -1 - j) for j in range(4)]
    near_slots, far_cells, far_weights, inverse = call(
        local_kernel,
        [(4 * lines, width)] * 3 + [block],
        send_cell, remap_weight, incoming_marine_slot, cells_sw, weights_sw, slots_sw,
    )
    (partial,) = call(flux_kernel, [block], forward[0], *forward_in, edge_in, near_slots)
    rhs, back, low, high = call(
        source_kernel, [block, (3 * lines, width), (24, width), (24, width)], partial, swap(partial), static[3]
    )
    rhs_in = [move(rhs, 1 + j, -1 - j) for j in range(4)]
    rhs_in += [move(back, -1, -5), move(low, -2, -6), move(high, 5, 1)]
    window = 6 * lines + 16
    send, keep = call(
        trace_kernel, [block, block], rhs, *rhs_in, static[3], *static_in, far_cells, far_weights,
        scratch=[pltpu.VMEM((window, width), F32)] * 3 + [pltpu.VMEM((window + 16, width), F32)] * 3,
    )
    return ((keep + swap(send)) * inverse)[None]


def solution(mesh):
    table = P(GRID, None)
    grid = P("comp", "tile", None)
    return jax.shard_map(
        shards,
        mesh=mesh,
        in_specs=(grid, grid, P("tile", None), table, table, table),
        out_specs=grid,
        check_vma=False,
    )
```

```python
import jax
import jax.experimental.pallas as pl
import jax.experimental.pallas.tpu as pltpu
import jax.numpy as jnp
from jax import lax
from jax.sharding import PartitionSpec as P

SPAN = 8
SWEEPS = 20
MIDDLE = SPAN // 2
F32 = jnp.float32
BF16 = jnp.bfloat16
I32 = jnp.int32
CONTRACT_LANES = (((1,), (1,)), ((), ()))
GRID = ("comp", "tile")


def call(kernel, shapes, *operands, scratch=(), where=pltpu.VMEM, flops=None):
    out = [jax.ShapeDtypeStruct(shape, F32) for shape in shapes]
    cost = None
    if flops is not None:
        cost = pl.CostEstimate(flops=flops, bytes_accessed=0, transcendentals=0)
    return pl.pallas_call(
        kernel,
        out_shape=out,
        in_specs=[pl.BlockSpec(memory_space=where)] * len(operands),
        out_specs=[pl.BlockSpec(memory_space=pltpu.VMEM)] * len(out),
        scratch_shapes=scratch,
        cost_estimate=cost,
        compiler_params=pltpu.CompilerParams(vmem_limit_bytes=32 * 1024 * 1024),
    )(*operands)


def on_each_component(atmosphere, ocean):
    comp = lax.axis_index("comp")
    pl.when(comp == 0)(atmosphere)
    pl.when(comp != 0)(ocean)


def fold(source, target, first):
    width = target.shape[1]
    lines = source.shape[1] // width
    for row in range(SPAN):
        for j in range(lines):
            piece = source[row : row + 1, j * width : (j + 1) * width]
            at = first + row * lines + j
            target[at : at + 1, :] = piece.astype(F32)


def gather_cells(table, index):
    rows, width = index.shape
    tiles = [(r, h) for r in range(0, rows, 8) for h in range(0, width, 128)]
    pieces = [index[r : r + 8, h : h + 128] for r, h in tiles]
    high = [lax.shift_right_logical(p, 7) for p in pieces]
    low = [p & 127 for p in pieces]
    found = [jnp.zeros((8, 128), F32) for _ in tiles]
    for i in range(rows * width // 128):
        r, h = divmod(i * 128, width)
        line = jnp.broadcast_to(table[r : r + 1, h : h + 128], (8, 128))
        for k in range(len(tiles)):
            picked = jnp.take_along_axis(line, low[k], axis=1, mode="promise_in_bounds")
            found[k] = jnp.where(high[k] == i, picked, found[k])
    across = width // 128
    return jnp.concatenate(
        [jnp.concatenate(found[k : k + across], 1) for k in range(0, len(found), across)], 0
    )


def scatter_add(total, values, index):
    rows, width = index.shape
    place = lax.broadcasted_iota(I32, (64, width), 0)
    for r in range(rows):
        cell = index[r : r + 1, :]
        value = values[r : r + 1, :]
        head = value.astype(BF16).astype(F32)
        tail = value - head
        row_here = place == lax.shift_right_logical(cell, 6)
        column_here = place == (cell & 63)
        spread = jnp.concatenate(
            [
                jnp.where(row_here, head, 0.0).astype(BF16),
                jnp.where(row_here, tail, 0.0).astype(BF16),
            ],
            0,
        )
        chosen = jnp.where(column_here, 1.0, 0.0).astype(BF16)
        total = total + lax.dot_general(
            spread, chosen, CONTRACT_LANES, preferred_element_type=F32
        )
    return total


def as_rows(total):
    both = total[:64] + total[64:]
    cells = both.reshape(16, 4, 64)
    return jnp.concatenate([cells[:, q, :] for q in range(4)], 1)


def pack_kernel(cells, weights, slots, state, coeff, vertical, pack, code, ints, reals, codes, sems):
    copies = [
        pltpu.make_async_copy(state.at[0], pack.at[256:272], sems.at[0]),
        pltpu.make_async_copy(coeff.at[0], pack.at[272:288], sems.at[1]),
        pltpu.make_async_copy(vertical, codes, sems.at[2]),
    ]
    for copy in copies:
        copy.start()

    def atmosphere():
        first = pltpu.make_async_copy(cells, ints, sems.at[3])
        second = pltpu.make_async_copy(weights, reals, sems.at[4])
        first.start()
        second.start()
        first.wait()
        fold(ints, pack, 0)
        second.wait()
        fold(reals, pack, 128)

    def ocean():
        first = pltpu.make_async_copy(slots, ints, sems.at[3])
        first.start()
        pack[128:256, :] = jnp.zeros((128, pack.shape[1]), F32)
        first.wait()
        fold(ints, pack, 0)

    on_each_component(atmosphere, ocean)
    for copy in copies:
        copy.wait()
    code[...] = codes[...].astype(F32)


def block_of(ref, k):
    return ref[16 * k : 16 * k + 16, :]


def message_kernel(pack, other, code, m1, m2, m3, m4, edge):
    def fill(air, sea, rows, rows_back):
        for j, m in enumerate((m1, m2, m3)):
            m[0:16, :] = block_of(air, rows[j])
            m[16:32, :] = block_of(air, 8 + rows[j])
            m[32:64, :] = air[256:288, :]
            m[64:80, :] = block_of(sea, rows_back[j])
            m[80:96, :] = sea[272:288, :]
            m[96:112, :] = code[...]
            m[112:128, :] = sea[256:272, :]
        m4[32:64, :] = air[256:288, :]
        m4[64:80, :] = sea[272:288, :]
        m4[80:96, :] = code[...]
        edge[...] = air[256:264, :]

    def atmosphere():
        fill(pack, other, (3, 2, 1), (5, 6, 7))
        m4[0:16, :] = block_of(pack, 0)
        m4[16:32, :] = block_of(pack, 8)

    def ocean():
        fill(other, pack, (5, 6, 7), (3, 2, 1))
        m4[0:16, :] = block_of(pack, 0)
        m4[16:32, :] = pack[256:272, :]

    on_each_component(atmosphere, ocean)


def share_kernel(pack, inverse):
    def atmosphere():
        total = jnp.zeros((128, 64), F32)
        for d in range(SPAN):
            total = scatter_add(total, block_of(pack, 8 + d), block_of(pack, d).astype(I32))
        inverse[...] = 1.0 / as_rows(total)

    def ocean():
        inverse[...] = jnp.ones_like(inverse)

    on_each_component(atmosphere, ocean)


def flux_kernel(edge, m1, m3, m2, m4, pack, other, partial):
    atmosphere = lax.axis_index("comp") == 0

    def part(k):
        rows = slice(16 * k, 16 * k + 16)
        local = block_of(other, (4, 12, 16, 17)[k])
        return [
            jnp.where(atmosphere, a[rows, :], b)
            for a, b in ((m1, local), (m2, m1[rows, :]), (m3, m2[rows, :]), (m4, m3[rows, :]))
        ]

    cells, weights, air, coeff = (part(k) for k in range(4))
    top = [a[0:1] for a in air]
    bottom = [a[15:16] for a in air]
    beyond = edge[0:1]
    total = jnp.zeros((128, 64), F32)
    for j in range(4):
        before = jnp.where(
            atmosphere,
            bottom[j - 1] if j else pack[271:272, :],
            bottom[j + 1] if j < 3 else m4[47:48, :],
        )
        after = jnp.where(atmosphere, top[j + 1] if j < 3 else beyond, top[j - 1] if j else beyond)
        s = air[j]
        near = jnp.concatenate([before, s[:-1]], 0) + jnp.concatenate([s[1:], after], 0)
        near = near + pltpu.roll(s, 1, 1) + pltpu.roll(s, s.shape[1] - 1, 1)
        flux = coeff[j] * (s + 0.2 * (near - 4.0 * s))
        picked = gather_cells(flux, cells[j].astype(I32))
        slot = jnp.where(atmosphere, block_of(other, 3 - j), block_of(pack, 4 + j)).astype(I32)
        total = scatter_add(total, weights[j] * picked, slot)
    partial[...] = as_rows(total)


def source_kernel(partial, partial_sw, pack, other, code, rhs, fifth, sixth):
    atmosphere = lax.axis_index("comp") == 0
    sea = jnp.where(atmosphere, other[256:272, :], pack[256:272, :])
    diagonal = jnp.where(atmosphere, other[272:288, :], pack[272:288, :])
    total = partial[...] + partial_sw[...] + sea
    rhs[...] = total
    for k, part in enumerate((total, diagonal, code[...])):
        fifth[16 * k : 16 * k + 16, :] = part
        sixth[8 * k : 8 * k + 8, :] = part[8:16]


def near_kernel(p1, p2, m1, m2, out):
    for k, (right, rows) in enumerate(((p1, slice(0, 16)), (m1, slice(80, 96)), (m1, slice(96, 112)))):
        out[16 * k : 16 * k + 16, :] = right[rows, :]
    for k, (right, rows) in enumerate(((p2, slice(8, 16)), (m2, slice(88, 96)), (m2, slice(104, 112)))):
        out[48 + 8 * k : 56 + 8 * k, :] = right[rows, :]


def edge_kernel(edge, out):
    out[...] = edge[...]


def trace_kernel(
    pack, other, inverse, own, near, fifth, sixth, p1, p2, p3, p4, m1, m2, m3, m4,
    send, keep, rhs, inv, code, code_up, code_down, eta,
):
    rows, width = rhs.shape
    groups = rows // 8

    def place(parts):
        at = 0
        for right, diagonal, face in parts:
            size = right.shape[0]
            rhs[at : at + size, :] = right[...]
            inv[at : at + size, :] = 1.0 / (diagonal[...] + 3.0)
            code[at : at + size, :] = face[...]
            at += size

    def thirds(ref, first, step, size):
        return [ref.at[first + k * step : first + k * step + size] for k in range(3)]

    others = [(p, m.at[80:96], m.at[96:112]) for p, m in ((p1, m1), (p2, m2), (p3, m3))]
    others.append((p4, m4.at[64:80], m4.at[80:96]))
    here = thirds(own, 0, 16, 16)
    on_each_component(
        lambda: place(
            [thirds(near, 48, 8, 8), thirds(near, 0, 16, 16), here, *others, thirds(fifth, 0, 16, 8)]
        ),
        lambda: place(
            [thirds(sixth, 0, 8, 8), thirds(fifth, 0, 16, 16), *others[::-1], here, thirds(near, 0, 16, 8)]
        ),
    )
    line = lax.broadcasted_iota(I32, (8, width), 0)

    def group(ref, g):
        return ref[8 * g : 8 * g + 8, :]

    def from_above(here, above):
        return jnp.where(line == 0, above, here)

    def from_below(here, below):
        return jnp.where(line == 7, below, here)

    downward = [pltpu.roll(group(code, g), 1, 0) for g in range(groups)]
    for g in range(groups):
        code_down[8 * g : 8 * g + 8, :] = from_above(downward[g], downward[max(g - 1, 0)])
    upward = [pltpu.roll(group(code, g), 7, 0) for g in range(groups)]
    for g in range(groups):
        code_up[8 * g : 8 * g + 8, :] = from_below(upward[g], upward[min(g + 1, groups - 1)])
    for g in range(groups):
        eta[8 * g : 8 * g + 8, :] = group(rhs, g) * group(inv, g)

    def sweep(step, carry):
        beside, above, below = {}, {}, {}

        def read(g):
            here = group(eta, g)
            left = pltpu.roll(here, 1, 1)
            right = pltpu.roll(here, width - 1, 1)
            beside[g] = left + right
            u, d = group(code_up, g), group(code_down, g)
            above[g] = pltpu.roll(jnp.where(u == 0.0, left, jnp.where(u == 1.0, here, right)), 1, 0)
            below[g] = pltpu.roll(jnp.where(d == 3.0, left, jnp.where(d == 4.0, here, right)), 7, 0)

        def write(g):
            up = from_above(above[g], above[max(g - 1, 0)])
            down = from_below(below[g], below[min(g + 1, groups - 1)])
            third = jnp.where(group(code, g) >= 3.0, down, up)
            eta[8 * g : 8 * g + 8, :] = (group(rhs, g) + (beside[g] + third)) * group(inv, g)

        for g in range(groups):
            read(g)
            if g:
                write(g - 1)
        write(groups - 1)
        return carry

    lax.fori_loop(1, SWEEPS, sweep, 0)

    atmosphere = lax.axis_index("comp") == 0
    sea = [jnp.where(atmosphere, other[256:272, :], m4[16:32, :])]
    slots = [jnp.where(atmosphere, block_of(other, 4), m4[0:16, :])]
    for a, b in ((m1, m3), (m2, m2), (m3, m1)):
        sea.append(jnp.where(atmosphere, a[112:128, :], b[112:128, :]))
        slots.append(jnp.where(atmosphere, a[64:80, :], b[64:80, :]))
    total = jnp.zeros((128, 64), F32)
    for i in range(4):
        at = 24 + 16 * i
        sst = 1.25 * sea[i] + 0.5 * eta[at : at + 16, :] - 0.25 * rhs[at : at + 16, :]
        picked = gather_cells(sst, slots[i].astype(I32))
        cell = jnp.where(atmosphere, block_of(pack, 4 + i), block_of(other, i)).astype(I32)
        weight = jnp.where(atmosphere, block_of(pack, 12 + i), block_of(other, 8 + i))
        total = scatter_add(total, weight * picked, cell)
    part = as_rows(total)
    send[...] = jnp.where(atmosphere, eta[24:40, :], part)
    keep[...] = jnp.where(atmosphere, part * inverse[...], 0.0)


def shards(state, coeff, vertical, send_cell, incoming_marine_slot, remap_weight):
    tiles = lax.axis_size("tile")
    block = state.shape[1:]
    lines, width = block

    def swap(x):
        return lax.ppermute(x, "comp", [(0, 1), (1, 0)])

    def move(x, atmosphere_from, ocean_from):
        pairs = [((t + atmosphere_from) % tiles, t) for t in range(tiles)]
        pairs += [(tiles + (t + ocean_from) % tiles, tiles + t) for t in range(tiles)]
        return lax.ppermute(x, GRID, pairs)

    arguments = (send_cell, remap_weight, incoming_marine_slot, state, coeff, vertical)
    pack, code = call(
        pack_kernel, [(18 * lines, width), block],
        *[pltpu.with_memory_space_constraint(x, pltpu.HBM) for x in arguments],
        scratch=[
            pltpu.VMEM(send_cell.shape, I32),
            pltpu.VMEM(send_cell.shape, F32),
            pltpu.VMEM(block, I32),
            pltpu.SemaphoreType.DMA((5,)),
        ],
        where=pltpu.HBM,
    )
    other = swap(pack)
    *messages, edge = call(
        message_kernel, [(8 * lines, width)] * 3 + [(6 * lines, width), (8, width)], pack, other, code
    )
    edge_in = move(edge, 5, 1)
    messages_in = [move(m, j, -j) for j, m in enumerate(messages, 1)]
    m1_in, m2_in, m3_in, m4_in = messages_in
    (inverse,) = call(share_kernel, [block], pack, flops=10**9)
    (edge_in,) = call(edge_kernel, [(8, width)], edge_in, flops=10**9)
    (partial,) = call(flux_kernel, [block], edge_in, m1_in, m3_in, m2_in, m4_in, pack, other)
    rhs, fifth, sixth = call(
        source_kernel, [block, (3 * lines, width), (24, width)], partial, swap(partial), pack, other, code
    )
    p1_in, p2_in, p3_in, p4_in = (move(rhs, j, -j) for j in range(1, 5))
    fifth_in = move(fifth, 5, -5)
    sixth_in = lax.ppermute(sixth, GRID, [(tiles + t, tiles + (t + 6) % tiles) for t in range(tiles)])
    (near,) = call(near_kernel, [(72, width)], p1_in, p2_in, m1_in, m2_in)
    window = (6 * lines + 16, width)
    send, keep = call(
        trace_kernel, [block, block],
        pack, other, inverse, fifth, swap(near), fifth_in, sixth_in, p1_in, p2_in, p3_in, p4_in, *messages_in,
        scratch=[pltpu.VMEM(window, F32)] * 6,
    )
    return (keep + swap(send) * inverse)[None]


def solution(mesh):
    table = P(GRID, None)
    grid = P("comp", "tile", None)
    return jax.shard_map(
        shards,
        mesh=mesh,
        in_specs=(grid, grid, P("tile", None), table, table, table),
        out_specs=grid,
        check_vma=False,
    )
```

```python
import jax
import jax.experimental.pallas as pl
import jax.experimental.pallas.tpu as pltpu
import jax.numpy as jnp
from jax import lax
from jax.sharding import PartitionSpec as P

SPAN = 8
SWEEPS = 20
MIDDLE = SPAN // 2
F32 = jnp.float32
BF16 = jnp.bfloat16
I32 = jnp.int32
CONTRACT_LANES = (((1,), (1,)), ((), ()))
GRID = ("comp", "tile")


def call(kernel, shapes, *operands, scratch=(), where=pltpu.VMEM, flops=None):
    out = [jax.ShapeDtypeStruct(shape, F32) for shape in shapes]
    cost = None
    if flops is not None:
        cost = pl.CostEstimate(flops=flops, bytes_accessed=0, transcendentals=0)
    return pl.pallas_call(
        kernel,
        out_shape=out,
        in_specs=[pl.BlockSpec(memory_space=where)] * len(operands),
        out_specs=[pl.BlockSpec(memory_space=pltpu.VMEM)] * len(out),
        scratch_shapes=scratch,
        cost_estimate=cost,
        compiler_params=pltpu.CompilerParams(vmem_limit_bytes=32 * 1024 * 1024),
    )(*operands)


def on_each_component(atmosphere, ocean):
    comp = lax.axis_index("comp")
    pl.when(comp == 0)(atmosphere)
    pl.when(comp != 0)(ocean)


def fold(source, target, first):
    width = target.shape[1]
    lines = source.shape[1] // width
    for row in range(SPAN):
        for j in range(lines):
            piece = source[row : row + 1, j * width : (j + 1) * width]
            at = first + row * lines + j
            target[at : at + 1, :] = piece.astype(F32)


def gather_cells(table, index):
    rows, width = index.shape
    tiles = [(r, h) for r in range(0, rows, 8) for h in range(0, width, 128)]
    pieces = [index[r : r + 8, h : h + 128] for r, h in tiles]
    high = [lax.shift_right_logical(p, 7) for p in pieces]
    low = [p & 127 for p in pieces]
    found = [jnp.zeros((8, 128), F32) for _ in tiles]
    for i in range(rows * width // 128):
        r, h = divmod(i * 128, width)
        line = jnp.broadcast_to(table[r : r + 1, h : h + 128], (8, 128))
        for k in range(len(tiles)):
            picked = jnp.take_along_axis(line, low[k], axis=1, mode="promise_in_bounds")
            found[k] = jnp.where(high[k] == i, picked, found[k])
    across = width // 128
    return jnp.concatenate(
        [jnp.concatenate(found[k : k + across], 1) for k in range(0, len(found), across)], 0
    )


def scatter_add(total, values, index):
    rows, width = index.shape
    place = lax.broadcasted_iota(I32, (64, width), 0)
    for r in range(rows):
        cell = index[r : r + 1, :]
        value = values[r : r + 1, :]
        head = value.astype(BF16).astype(F32)
        tail = value - head
        row_here = place == lax.shift_right_logical(cell, 6)
        column_here = place == (cell & 63)
        spread = jnp.concatenate(
            [
                jnp.where(row_here, head, 0.0).astype(BF16),
                jnp.where(row_here, tail, 0.0).astype(BF16),
            ],
            0,
        )
        chosen = jnp.where(column_here, 1.0, 0.0).astype(BF16)
        total = total + lax.dot_general(
            spread, chosen, CONTRACT_LANES, preferred_element_type=F32
        )
    return total


def as_rows(total):
    both = total[:64] + total[64:]
    cells = both.reshape(16, 4, 64)
    return jnp.concatenate([cells[:, q, :] for q in range(4)], 1)


def pack_kernel(cells, weights, slots, state, coeff, vertical, pack, code, ints, reals, codes, sems):
    copies = [
        pltpu.make_async_copy(state.at[0], pack.at[256:272], sems.at[0]),
        pltpu.make_async_copy(coeff.at[0], pack.at[272:288], sems.at[1]),
        pltpu.make_async_copy(vertical, codes, sems.at[2]),
    ]
    for copy in copies:
        copy.start()

    def atmosphere():
        first = pltpu.make_async_copy(cells, ints, sems.at[3])
        second = pltpu.make_async_copy(weights, reals, sems.at[4])
        first.start()
        second.start()
        first.wait()
        fold(ints, pack, 0)
        second.wait()
        fold(reals, pack, 128)

    def ocean():
        first = pltpu.make_async_copy(slots, ints, sems.at[3])
        first.start()
        pack[128:256, :] = jnp.zeros((128, pack.shape[1]), F32)
        first.wait()
        fold(ints, pack, 0)

    on_each_component(atmosphere, ocean)
    for copy in copies:
        copy.wait()
    code[...] = codes[...].astype(F32)


def block_of(ref, k):
    return ref[16 * k : 16 * k + 16]


def message_kernel(pack, other, code, m1, m2, m3, m4, edge):
    def fill(air, sea, rows, rows_back):
        s = air[256:272, :]
        coeff = air[272:288, :]
        none = jnp.zeros_like(s[0:1])
        near = jnp.concatenate([none, s[:-1]], 0) + jnp.concatenate([s[1:], none], 0)
        near = near + pltpu.roll(s, 1, 1) + pltpu.roll(s, s.shape[1] - 1, 1)
        flux = coeff * (s + 0.2 * (near - 4.0 * s))
        ends = jnp.concatenate([coeff[0:1], coeff[15:16], s[0:1], s[15:16], none, none, none, none], 0)
        for j, m in enumerate((m1, m2, m3)):
            m[0:16, :] = block_of(air, rows[j])
            m[16:32, :] = block_of(air, 8 + rows[j])
            m[32:48, :] = flux
            m[48:64, :] = block_of(sea, rows_back[j])
            m[64:72, :] = ends
            m[72:88, :] = sea[272:288, :]
            m[88:104, :] = code[...]
            m[104:120, :] = sea[256:272, :]
        m4[32:48, :] = flux
        m4[48:56, :] = ends
        m4[56:72, :] = sea[272:288, :]
        m4[72:88, :] = code[...]
        edge[...] = s[0:8]

    def atmosphere():
        fill(pack, other, (3, 2, 1), (5, 6, 7))
        m4[0:16, :] = block_of(pack, 0)
        m4[16:32, :] = block_of(pack, 8)

    def ocean():
        fill(other, pack, (5, 6, 7), (3, 2, 1))
        m4[0:16, :] = block_of(pack, 0)
        m4[16:32, :] = pack[256:272, :]

    on_each_component(atmosphere, ocean)


def share_kernel(pack, inverse):
    def atmosphere():
        total = jnp.zeros((128, 64), F32)
        for d in range(SPAN):
            total = scatter_add(total, block_of(pack, 8 + d), block_of(pack, d).astype(I32))
        inverse[...] = 1.0 / as_rows(total)

    def ocean():
        inverse[...] = jnp.ones_like(inverse)

    on_each_component(atmosphere, ocean)


def edge_kernel(edge, out):
    out[...] = edge[...]


def add_fluxes(total, cells, weights, flux, ends, before, after, slots):
    first = flux[0:1] + ends[0:1] * (0.2 * before)
    last = flux[15:16] + ends[1:2] * (0.2 * after)
    flux = jnp.concatenate([first, flux[1:15], last], 0)
    return scatter_add(total, weights * gather_cells(flux, cells.astype(I32)), slots.astype(I32))


def flux_kernel(edge, m1, m2, m3, m4, own, pack, other, partial):
    atmosphere = lax.axis_index("comp") == 0

    def either(a, b):
        return jnp.where(atmosphere, a, b)

    def part(m):
        return m[0:16, :], m[16:32, :], m[32:48, :], m[64:72, :]

    total = jnp.zeros((128, 64), F32)
    before = either(pack[271:272, :], m2[67:68, :])
    after = either(m2[66:67, :], other[256:257, :])
    total = add_fluxes(total, *part(m1), before, after, either(block_of(other, 3), block_of(pack, 5)))
    before = either(m1[67:68, :], m3[67:68, :])
    after = either(m3[66:67, :], m1[66:67, :])
    total = add_fluxes(total, *part(m2), before, after, either(block_of(other, 2), block_of(pack, 6)))
    before = either(m2[67:68, :], m4[51:52, :])
    after = either(m4[50:51, :], m2[66:67, :])
    total = add_fluxes(total, *part(m3), before, after, either(block_of(other, 1), block_of(pack, 7)))
    before = either(m3[67:68, :], m1[67:68, :])
    cells = either(m4[0:16, :], block_of(other, 4))
    weights = either(m4[16:32, :], block_of(other, 12))
    flux = either(m4[32:48, :], own[32:48, :])
    ends = either(m4[48:56, :], own[64:72, :])
    slots = either(block_of(other, 0), block_of(pack, 4))
    partial[...] = as_rows(add_fluxes(total, cells, weights, flux, ends, before, edge[0:1, :], slots))


def source_kernel(partial, partial_sw, pack, other, code, rhs, fifth, sixth):
    atmosphere = lax.axis_index("comp") == 0
    sea = jnp.where(atmosphere, other[256:272, :], pack[256:272, :])
    diagonal = jnp.where(atmosphere, other[272:288, :], pack[272:288, :])
    total = partial[...] + partial_sw[...] + sea
    rhs[...] = total
    for k, part in enumerate((total, diagonal, code[...])):
        fifth[16 * k : 16 * k + 16, :] = part
        sixth[8 * k : 8 * k + 8, :] = part[8:16]


def near_kernel(p1, p2, m1, m2, out):
    out[0:16, :] = p1[...]
    out[16:48, :] = m1[72:104, :]
    out[48:56, :] = p2[8:16, :]
    out[56:64, :] = m2[80:88, :]
    out[64:72, :] = m2[96:104, :]


def trace_kernel(
    pack, other, inverse, own, near, fifth, sixth, p1, p2, p3, p4, m1, m2, m3, m4,
    send, keep, rhs, inv, code, code_up, code_down, eta,
):
    rows, width = rhs.shape
    groups = rows // 8

    def place(parts):
        at = 0
        for right, diagonal, face in parts:
            size = right.shape[0]
            rhs[at : at + size, :] = right[...]
            inv[at : at + size, :] = 1.0 / (diagonal[...] + 3.0)
            code[at : at + size, :] = face[...]
            at += size

    def thirds(ref, first, step, size):
        return [ref.at[first + k * step : first + k * step + size] for k in range(3)]

    others = [(p, m.at[72:88], m.at[88:104]) for p, m in ((p1, m1), (p2, m2), (p3, m3))]
    others.append((p4, m4.at[56:72], m4.at[72:88]))
    here = thirds(own, 0, 16, 16)
    on_each_component(
        lambda: place(
            [thirds(near, 48, 8, 8), thirds(near, 0, 16, 16), here, *others, thirds(fifth, 0, 16, 8)]
        ),
        lambda: place(
            [thirds(sixth, 0, 8, 8), thirds(fifth, 0, 16, 16), *others[::-1], here, thirds(near, 0, 16, 8)]
        ),
    )
    line = lax.broadcasted_iota(I32, (8, width), 0)

    def group(ref, g):
        return ref[8 * g : 8 * g + 8, :]

    def from_above(here, above):
        return jnp.where(line == 0, above, here)

    def from_below(here, below):
        return jnp.where(line == 7, below, here)

    downward = [pltpu.roll(group(code, g), 1, 0) for g in range(groups)]
    for g in range(groups):
        code_down[8 * g : 8 * g + 8, :] = from_above(downward[g], downward[max(g - 1, 0)])
    upward = [pltpu.roll(group(code, g), 7, 0) for g in range(groups)]
    for g in range(groups):
        code_up[8 * g : 8 * g + 8, :] = from_below(upward[g], upward[min(g + 1, groups - 1)])
    for g in range(groups):
        eta[8 * g : 8 * g + 8, :] = group(rhs, g) * group(inv, g)

    def sweep(first, last):
        beside, above, below = {}, {}, {}

        def read(g):
            here = group(eta, g)
            left = pltpu.roll(here, 1, 1)
            right = pltpu.roll(here, width - 1, 1)
            beside[g] = left + right
            u, d = group(code_up, g), group(code_down, g)
            above[g] = pltpu.roll(jnp.where(u == 0.0, left, jnp.where(u == 1.0, here, right)), 1, 0)
            below[g] = pltpu.roll(jnp.where(d == 3.0, left, jnp.where(d == 4.0, here, right)), 7, 0)

        def write(g):
            up = from_above(above[g], above[max(g - 1, first)])
            down = from_below(below[g], below[min(g + 1, last - 1)])
            third = jnp.where(group(code, g) >= 3.0, down, up)
            eta[8 * g : 8 * g + 8, :] = (group(rhs, g) + (beside[g] + third)) * group(inv, g)

        for g in range(first, last):
            read(g)
            if g > first:
                write(g - 1)
        write(last - 1)

    def repeat(count, skip):
        def several(_, carry):
            for _ in range(4):
                sweep(skip, groups - skip)
            return carry

        for _ in range(count % 4):
            sweep(skip, groups - skip)
        if count >= 4:
            lax.fori_loop(0, count // 4, several, 0)

    done = 1
    for skip in range(3):
        until = min(SWEEPS, SWEEPS - 16 + 8 * skip)
        repeat(until - done, skip)
        done = until

    atmosphere = lax.axis_index("comp") == 0
    states = [m[104:120, :] for m in (m1, m2, m3)]
    sea = [jnp.where(atmosphere, other[256:272, :], m4[16:32, :])]
    sea += [jnp.where(atmosphere, states[i], states[2 - i]) for i in range(3)]
    slots = [jnp.where(atmosphere, block_of(other, 4), m4[0:16, :])]
    for a, b in ((m1, m3), (m2, m2), (m3, m1)):
        slots.append(jnp.where(atmosphere, a[48:64, :], b[48:64, :]))
    total = jnp.zeros((128, 64), F32)
    for i in range(4):
        at = 24 + 16 * i
        sst = 1.25 * sea[i] + 0.5 * eta[at : at + 16, :] - 0.25 * rhs[at : at + 16, :]
        picked = gather_cells(sst, slots[i].astype(I32))
        cell = jnp.where(atmosphere, block_of(pack, 4 + i), block_of(other, i)).astype(I32)
        weight = jnp.where(atmosphere, block_of(pack, 12 + i), block_of(other, 8 + i))
        total = scatter_add(total, weight * picked, cell)
    part = as_rows(total)
    send[...] = jnp.where(atmosphere, eta[24:40, :], part)
    keep[...] = jnp.where(atmosphere, part * inverse[...], 0.0)


def shards(state, coeff, vertical, send_cell, incoming_marine_slot, remap_weight):
    tiles = lax.axis_size("tile")
    block = state.shape[1:]
    lines, width = block

    def swap(x):
        return lax.ppermute(x, "comp", [(0, 1), (1, 0)])

    def move(x, atmosphere_from, ocean_from):
        pairs = [((t + atmosphere_from) % tiles, t) for t in range(tiles)]
        pairs += [(tiles + (t + ocean_from) % tiles, tiles + t) for t in range(tiles)]
        return lax.ppermute(x, GRID, pairs)

    arguments = (send_cell, remap_weight, incoming_marine_slot, state, coeff, vertical)
    pack, code = call(
        pack_kernel, [(18 * lines, width), block],
        *[pltpu.with_memory_space_constraint(x, pltpu.HBM) for x in arguments],
        scratch=[
            pltpu.VMEM(send_cell.shape, I32),
            pltpu.VMEM(send_cell.shape, F32),
            pltpu.VMEM(block, I32),
            pltpu.SemaphoreType.DMA((5,)),
        ],
        where=pltpu.HBM,
    )
    other = swap(pack)
    tall = 4 * lines + 8
    *messages, edge = call(
        message_kernel,
        [(tall + 3 * lines, width)] * 3 + [(tall + lines, width), (8, width)],
        pack, other, code,
    )
    (edge_in,) = call(edge_kernel, [(8, width)], move(edge, 5, 1), flops=10**9)
    m1_in, m2_in, m3_in, m4_in = messages_in = [move(m, j, -j) for j, m in enumerate(messages, 1)]
    (inverse,) = call(share_kernel, [block], pack, flops=10**9)
    (partial,) = call(flux_kernel, [block], edge_in, *messages_in, messages[1], pack, other, flops=10**9)
    rhs, fifth, sixth = call(
        source_kernel, [block, (3 * lines, width), (24, width)], partial, swap(partial), pack, other, code
    )
    p1_in, p2_in, p3_in, p4_in = (move(rhs, j, -j) for j in range(1, 5))
    fifth_in = move(fifth, 5, -5)
    sixth_in = lax.ppermute(sixth, GRID, [(tiles + t, tiles + (t + 6) % tiles) for t in range(tiles)])
    (near,) = call(near_kernel, [(72, width)], p1_in, p2_in, m1_in, m2_in)
    window = (6 * lines + 16, width)
    send, keep = call(
        trace_kernel, [block, block],
        pack, other, inverse, fifth, swap(near), fifth_in, sixth_in, p1_in, p2_in, p3_in, p4_in, *messages_in,
        scratch=[pltpu.VMEM(window, F32)] * 6,
    )
    return (keep + swap(send) * inverse)[None]


def solution(mesh):
    table = P(GRID, None)
    grid = P("comp", "tile", None)
    return jax.shard_map(
        shards,
        mesh=mesh,
        in_specs=(grid, grid, P("tile", None), table, table, table),
        out_specs=grid,
        check_vma=False,
    )
```

```python
import jax
import jax.experimental.pallas as pl
import jax.experimental.pallas.tpu as pltpu
import jax.numpy as jnp
from jax import lax
from jax.sharding import PartitionSpec as P

SPAN = 8
SWEEPS = 20
MIDDLE = SPAN // 2
F32 = jnp.float32
BF16 = jnp.bfloat16
I32 = jnp.int32
CONTRACT_LANES = (((1,), (1,)), ((), ()))
GRID = ("comp", "tile")


def call(kernel, shapes, *operands, scratch=(), where=pltpu.VMEM, flops=None):
    out = [jax.ShapeDtypeStruct(shape, F32) for shape in shapes]
    cost = None
    if flops is not None:
        cost = pl.CostEstimate(flops=flops, bytes_accessed=0, transcendentals=0)
    return pl.pallas_call(
        kernel,
        out_shape=out,
        in_specs=[pl.BlockSpec(memory_space=where)] * len(operands),
        out_specs=[pl.BlockSpec(memory_space=pltpu.VMEM)] * len(out),
        scratch_shapes=scratch,
        cost_estimate=cost,
        compiler_params=pltpu.CompilerParams(vmem_limit_bytes=32 * 1024 * 1024),
    )(*operands)


def on_each_component(atmosphere, ocean):
    comp = lax.axis_index("comp")
    pl.when(comp == 0)(atmosphere)
    pl.when(comp != 0)(ocean)


def fold(source, target, first):
    width = target.shape[1]
    lines = source.shape[1] // width
    for row in range(SPAN):
        for j in range(lines):
            piece = source[row : row + 1, j * width : (j + 1) * width]
            at = first + row * lines + j
            target[at : at + 1, :] = piece.astype(F32)


def gather_cells(table, index):
    rows, width = index.shape
    tiles = [(r, h) for r in range(0, rows, 8) for h in range(0, width, 128)]
    pieces = [index[r : r + 8, h : h + 128] for r, h in tiles]
    high = [lax.shift_right_logical(p, 7) for p in pieces]
    low = [p & 127 for p in pieces]
    found = [jnp.zeros((8, 128), F32) for _ in tiles]
    for i in range(rows * width // 128):
        r, h = divmod(i * 128, width)
        line = jnp.broadcast_to(table[r : r + 1, h : h + 128], (8, 128))
        for k in range(len(tiles)):
            picked = jnp.take_along_axis(line, low[k], axis=1, mode="promise_in_bounds")
            found[k] = jnp.where(high[k] == i, picked, found[k])
    across = width // 128
    return jnp.concatenate(
        [jnp.concatenate(found[k : k + across], 1) for k in range(0, len(found), across)], 0
    )


def scatter_add(total, values, index):
    rows, width = index.shape
    place = lax.broadcasted_iota(I32, (64, width), 0)
    for r in range(rows):
        cell = index[r : r + 1, :]
        value = values[r : r + 1, :]
        head = value.astype(BF16).astype(F32)
        tail = value - head
        row_here = place == lax.shift_right_logical(cell, 6)
        column_here = place == (cell & 63)
        spread = jnp.concatenate(
            [
                jnp.where(row_here, head, 0.0).astype(BF16),
                jnp.where(row_here, tail, 0.0).astype(BF16),
            ],
            0,
        )
        chosen = jnp.where(column_here, 1.0, 0.0).astype(BF16)
        total = total + lax.dot_general(
            spread, chosen, CONTRACT_LANES, preferred_element_type=F32
        )
    return total


def as_rows(total):
    both = total[:64] + total[64:]
    cells = both.reshape(16, 4, 64)
    return jnp.concatenate([cells[:, q, :] for q in range(4)], 1)


def pack_kernel(cells, weights, slots, state, coeff, vertical, pack, code, ints, reals, codes, sems):
    copies = [
        pltpu.make_async_copy(state.at[0], pack.at[256:272], sems.at[0]),
        pltpu.make_async_copy(coeff.at[0], pack.at[272:288], sems.at[1]),
        pltpu.make_async_copy(vertical, codes, sems.at[2]),
    ]
    for copy in copies:
        copy.start()

    def atmosphere():
        first = pltpu.make_async_copy(cells, ints, sems.at[3])
        second = pltpu.make_async_copy(weights, reals, sems.at[4])
        first.start()
        second.start()
        first.wait()
        fold(ints, pack, 0)
        second.wait()
        fold(reals, pack, 128)

    def ocean():
        first = pltpu.make_async_copy(slots, ints, sems.at[3])
        first.start()
        pack[128:256, :] = jnp.zeros((128, pack.shape[1]), F32)
        first.wait()
        ints[...] = renumbered(ints[...])
        fold(ints, pack, 0)

    on_each_component(atmosphere, ocean)
    for copy in copies:
        copy.wait()
    code[...] = halved(codes[...].astype(F32))

    @pl.when(lax.axis_index("comp") != 0)
    def _():
        pack[256:272, :] = halved(pack[256:272, :])
        pack[272:288, :] = halved(pack[272:288, :])


def halved(x):
    width = x.shape[1] // 2
    a, b = x[:, :width], x[:, width:]
    lane = lax.broadcasted_iota(I32, a.shape, 1)

    def picked(odd):
        index = ((2 * lane) & (width - 1)) + odd
        first = jnp.take_along_axis(a, index, axis=1, mode="promise_in_bounds")
        second = jnp.take_along_axis(b, index, axis=1, mode="promise_in_bounds")
        return jnp.where(lane < width // 2, first, second)

    return jnp.concatenate([picked(0), picked(1)], 1)


def unhalved(a, b):
    lane = lax.broadcasted_iota(I32, a.shape, 1)
    width = a.shape[1]

    def picked(first):
        index = lax.shift_right_logical(lane, 1) + first
        even = jnp.take_along_axis(a, index, axis=1, mode="promise_in_bounds")
        odd = jnp.take_along_axis(b, index, axis=1, mode="promise_in_bounds")
        return jnp.where((lane & 1) == 0, even, odd)

    return jnp.concatenate([picked(0), picked(width // 2)], 1)


def renumbered(cell):
    return (cell & ~255) + lax.shift_left(cell & 1, 7) + lax.shift_right_logical(cell & 255, 1)


def block_of(ref, k):
    return ref[16 * k : 16 * k + 16]


def message_kernel(pack, other, code, m1, m2, m3, m4, edge):
    def fill(air, sea, rows, rows_back):
        s = air[256:272, :]
        coeff = air[272:288, :]
        none = jnp.zeros_like(s[0:1])
        near = jnp.concatenate([none, s[:-1]], 0) + jnp.concatenate([s[1:], none], 0)
        near = near + pltpu.roll(s, 1, 1) + pltpu.roll(s, s.shape[1] - 1, 1)
        flux = coeff * (s + 0.2 * (near - 4.0 * s))
        ends = jnp.concatenate([coeff[0:1], coeff[15:16], s[0:1], s[15:16], none, none, none, none], 0)
        for j, m in enumerate((m1, m2, m3)):
            m[0:16, :] = block_of(air, rows[j])
            m[16:32, :] = block_of(air, 8 + rows[j])
            m[32:48, :] = flux
            m[48:64, :] = block_of(sea, rows_back[j])
            m[64:72, :] = ends
            m[72:88, :] = sea[272:288, :]
            m[88:104, :] = code[...]
            m[104:120, :] = sea[256:272, :]
        m4[32:48, :] = flux
        m4[48:56, :] = ends
        m4[56:72, :] = sea[272:288, :]
        m4[72:88, :] = code[...]
        edge[...] = s[0:8]

    def atmosphere():
        fill(pack, other, (3, 2, 1), (5, 6, 7))
        m4[0:16, :] = block_of(pack, 0)
        m4[16:32, :] = block_of(pack, 8)

    def ocean():
        fill(other, pack, (5, 6, 7), (3, 2, 1))
        m4[0:16, :] = block_of(pack, 0)
        m4[16:32, :] = pack[256:272, :]

    on_each_component(atmosphere, ocean)


def share_kernel(pack, inverse):
    def atmosphere():
        total = jnp.zeros((128, 64), F32)
        for d in range(SPAN):
            total = scatter_add(total, block_of(pack, 8 + d), block_of(pack, d).astype(I32))
        inverse[...] = 1.0 / as_rows(total)

    def ocean():
        inverse[...] = jnp.ones_like(inverse)

    on_each_component(atmosphere, ocean)


def edge_kernel(edge, out):
    out[...] = edge[...]


def add_fluxes(total, cells, weights, flux, ends, before, after, slots):
    first = flux[0:1] + ends[0:1] * (0.2 * before)
    last = flux[15:16] + ends[1:2] * (0.2 * after)
    flux = jnp.concatenate([first, flux[1:15], last], 0)
    return scatter_add(total, weights * gather_cells(flux, cells.astype(I32)), slots.astype(I32))


def flux_kernel(edge, m1, m2, m3, m4, own, pack, other, partial):
    atmosphere = lax.axis_index("comp") == 0

    def either(a, b):
        return jnp.where(atmosphere, a, b)

    def part(m):
        return m[0:16, :], m[16:32, :], m[32:48, :], m[64:72, :]

    total = jnp.zeros((128, 64), F32)
    before = either(pack[271:272, :], m2[67:68, :])
    after = either(m2[66:67, :], other[256:257, :])
    total = add_fluxes(total, *part(m1), before, after, either(block_of(other, 3), block_of(pack, 5)))
    before = either(m1[67:68, :], m3[67:68, :])
    after = either(m3[66:67, :], m1[66:67, :])
    total = add_fluxes(total, *part(m2), before, after, either(block_of(other, 2), block_of(pack, 6)))
    before = either(m2[67:68, :], m4[51:52, :])
    after = either(m4[50:51, :], m2[66:67, :])
    total = add_fluxes(total, *part(m3), before, after, either(block_of(other, 1), block_of(pack, 7)))
    before = either(m3[67:68, :], m1[67:68, :])
    cells = either(m4[0:16, :], block_of(other, 4))
    weights = either(m4[16:32, :], block_of(other, 12))
    flux = either(m4[32:48, :], own[32:48, :])
    ends = either(m4[48:56, :], own[64:72, :])
    slots = either(block_of(other, 0), block_of(pack, 4))
    partial[...] = as_rows(add_fluxes(total, cells, weights, flux, ends, before, edge[0:1, :], slots))


def source_kernel(partial, partial_sw, pack, other, code, rhs, fifth, sixth):
    atmosphere = lax.axis_index("comp") == 0
    sea = jnp.where(atmosphere, other[256:272, :], pack[256:272, :])
    diagonal = jnp.where(atmosphere, other[272:288, :], pack[272:288, :])
    total = partial[...] + partial_sw[...] + sea
    rhs[...] = total
    for k, part in enumerate((total, diagonal, code[...])):
        fifth[16 * k : 16 * k + 16, :] = part
        sixth[8 * k : 8 * k + 8, :] = part[8:16]


def near_kernel(p1, p2, m1, m2, out):
    out[0:16, :] = p1[...]
    out[16:48, :] = m1[72:104, :]
    out[48:56, :] = p2[8:16, :]
    out[56:64, :] = m2[80:88, :]
    out[64:72, :] = m2[96:104, :]


def trace_kernel(
    pack, other, inverse, own, near, fifth, sixth, p1, p2, p3, p4, m1, m2, m3, m4,
    send, keep, rhs, inv, code, code_up, code_down, even, odd,
):
    rows, width = rhs.shape
    groups = rows // 8

    def place(parts):
        at = 0
        for right, diagonal, face in parts:
            size = right.shape[0]
            rhs[at : at + size, :] = right[...]
            inv[at : at + size, :] = 1.0 / (diagonal[...] + 3.0)
            code[at : at + size, :] = face[...]
            at += size

    def thirds(ref, first, step, size):
        return [ref.at[first + k * step : first + k * step + size] for k in range(3)]

    others = [(p, m.at[72:88], m.at[88:104]) for p, m in ((p1, m1), (p2, m2), (p3, m3))]
    others.append((p4, m4.at[56:72], m4.at[72:88]))
    here = thirds(own, 0, 16, 16)
    on_each_component(
        lambda: place(
            [thirds(near, 48, 8, 8), thirds(near, 0, 16, 16), here, *others, thirds(fifth, 0, 16, 8)]
        ),
        lambda: place(
            [thirds(sixth, 0, 8, 8), thirds(fifth, 0, 16, 16), *others[::-1], here, thirds(near, 0, 16, 8)]
        ),
    )
    line = lax.broadcasted_iota(I32, (8, width), 0)

    def group(ref, g):
        return ref[8 * g : 8 * g + 8, :]

    def from_above(here, above):
        return jnp.where(line[:, : here.shape[1]] == 0, above, here)

    def from_below(here, below):
        return jnp.where(line[:, : here.shape[1]] == 7, below, here)

    downward = [pltpu.roll(group(code, g), 1, 0) for g in range(groups)]
    for g in range(groups):
        code_down[8 * g : 8 * g + 8, :] = from_above(downward[g], downward[max(g - 1, 0)])
    upward = [pltpu.roll(group(code, g), 7, 0) for g in range(groups)]
    for g in range(groups):
        code_up[8 * g : 8 * g + 8, :] = from_below(upward[g], upward[min(g + 1, groups - 1)])
    half = width // 2
    for g in range(groups):
        first = group(rhs, g) * group(inv, g)
        even[8 * g : 8 * g + 8, :] = first[:, :half]
        odd[8 * g : 8 * g + 8, :] = first[:, half:]

    def sweep(first, last):
        beside, above, below = {}, {}, {}

        def chosen(code, zero, left, here, right):
            return jnp.where(code == zero, left, jnp.where(code == zero + 1.0, here, right))

        def read(g):
            e, o = group(even, g), group(odd, g)
            left = pltpu.roll(o, 1, 1)
            right = pltpu.roll(e, half - 1, 1)
            beside[g] = left + o, e + right
            u, d = group(code_up, g), group(code_down, g)
            up = (chosen(u[:, :half], 0.0, left, e, o), chosen(u[:, half:], 0.0, e, o, right))
            down = (chosen(d[:, :half], 3.0, left, e, o), chosen(d[:, half:], 3.0, e, o, right))
            above[g] = [pltpu.roll(x, 1, 0) for x in up]
            below[g] = [pltpu.roll(x, 7, 0) for x in down]

        def write(g):
            for k, ref in enumerate((even, odd)):
                lanes = slice(k * half, k * half + half)
                up = from_above(above[g][k], above[max(g - 1, first)][k])
                down = from_below(below[g][k], below[min(g + 1, last - 1)][k])
                third = jnp.where(group(code, g)[:, lanes] >= 3.0, down, up)
                total = group(rhs, g)[:, lanes] + (beside[g][k] + third)
                ref[8 * g : 8 * g + 8, :] = total * group(inv, g)[:, lanes]

        for g in range(first, last):
            read(g)
            if g > first:
                write(g - 1)
        write(last - 1)

    def repeat(count, skip):
        def several(_, carry):
            for _ in range(8):
                sweep(skip, groups - skip)
            return carry

        for _ in range(count % 8):
            sweep(skip, groups - skip)
        if count >= 8:
            lax.fori_loop(0, count // 8, several, 0)

    done = 1
    for skip in range(3):
        until = min(SWEEPS, SWEEPS - 16 + 8 * skip)
        repeat(until - done, skip)
        done = until

    atmosphere = lax.axis_index("comp") == 0
    states = [m[104:120, :] for m in (m1, m2, m3)]
    sea = [jnp.where(atmosphere, other[256:272, :], m4[16:32, :])]
    sea += [jnp.where(atmosphere, states[i], states[2 - i]) for i in range(3)]
    slots = [jnp.where(atmosphere, block_of(other, 4), m4[0:16, :])]
    for a, b in ((m1, m3), (m2, m2), (m3, m1)):
        slots.append(jnp.where(atmosphere, a[48:64, :], b[48:64, :]))
    total = jnp.zeros((128, 64), F32)
    for i in range(4):
        at = 24 + 16 * i
        eta = jnp.concatenate([even[at : at + 16, :], odd[at : at + 16, :]], 1)
        sst = 1.25 * sea[i] + 0.5 * eta - 0.25 * rhs[at : at + 16, :]
        picked = gather_cells(sst, slots[i].astype(I32))
        cell = jnp.where(atmosphere, block_of(pack, 4 + i), block_of(other, i)).astype(I32)
        weight = jnp.where(atmosphere, block_of(pack, 12 + i), block_of(other, 8 + i))
        total = scatter_add(total, weight * picked, cell)
    part = as_rows(total)
    send[...] = jnp.where(atmosphere, unhalved(even[24:40, :], odd[24:40, :]), part)
    keep[...] = jnp.where(atmosphere, part * inverse[...], 0.0)


def shards(state, coeff, vertical, send_cell, incoming_marine_slot, remap_weight):
    tiles = lax.axis_size("tile")
    block = state.shape[1:]
    lines, width = block

    def swap(x):
        return lax.ppermute(x, "comp", [(0, 1), (1, 0)])

    def move(x, atmosphere_from, ocean_from):
        pairs = [((t + atmosphere_from) % tiles, t) for t in range(tiles)]
        pairs += [(tiles + (t + ocean_from) % tiles, tiles + t) for t in range(tiles)]
        return lax.ppermute(x, GRID, pairs)

    arguments = (send_cell, remap_weight, incoming_marine_slot, state, coeff, vertical)
    pack, code = call(
        pack_kernel, [(18 * lines, width), block],
        *[pltpu.with_memory_space_constraint(x, pltpu.HBM) for x in arguments],
        scratch=[
            pltpu.VMEM(send_cell.shape, I32),
            pltpu.VMEM(send_cell.shape, F32),
            pltpu.VMEM(block, I32),
            pltpu.SemaphoreType.DMA((5,)),
        ],
        where=pltpu.HBM,
    )
    other = swap(pack)
    tall = 4 * lines + 8
    *messages, edge = call(
        message_kernel,
        [(tall + 3 * lines, width)] * 3 + [(tall + lines, width), (8, width)],
        pack, other, code,
    )
    (edge_in,) = call(edge_kernel, [(8, width)], move(edge, 5, 1), flops=10**9)
    m1_in, m2_in, m3_in, m4_in = messages_in = [move(m, j, -j) for j, m in enumerate(messages, 1)]
    (inverse,) = call(share_kernel, [block], pack, flops=10**9)
    (partial,) = call(flux_kernel, [block], edge_in, *messages_in, messages[1], pack, other, flops=10**9)
    rhs, fifth, sixth = call(
        source_kernel, [block, (3 * lines, width), (24, width)], partial, swap(partial), pack, other, code
    )
    p1_in, p2_in, p3_in, p4_in = (move(rhs, j, -j) for j in range(1, 5))
    fifth_in = move(fifth, 5, -5)
    sixth_in = lax.ppermute(sixth, GRID, [(tiles + t, tiles + (t + 6) % tiles) for t in range(tiles)])
    (near,) = call(near_kernel, [(72, width)], p1_in, p2_in, m1_in, m2_in)
    window = (6 * lines + 16, width)
    send, keep = call(
        trace_kernel, [block, block],
        pack, other, inverse, fifth, swap(near), fifth_in, sixth_in, p1_in, p2_in, p3_in, p4_in, *messages_in,
        scratch=[pltpu.VMEM(window, F32)] * 5
        + [pltpu.VMEM((window[0], width // 2), F32)] * 2,
    )
    return (keep + swap(send) * inverse)[None]


def solution(mesh):
    table = P(GRID, None)
    grid = P("comp", "tile", None)
    return jax.shard_map(
        shards,
        mesh=mesh,
        in_specs=(grid, grid, P("tile", None), table, table, table),
        out_specs=grid,
        check_vma=False,
    )
```

```python
import jax
import jax.experimental.pallas as pl
import jax.experimental.pallas.tpu as pltpu
import jax.numpy as jnp
from jax import lax
from jax.sharding import PartitionSpec as P

SPAN = 8
SWEEPS = 20
MIDDLE = SPAN // 2
F32 = jnp.float32
BF16 = jnp.bfloat16
I32 = jnp.int32
CONTRACT_LANES = (((1,), (1,)), ((), ()))
GRID = ("comp", "tile")


def call(kernel, shapes, *operands, scratch=(), where=pltpu.VMEM, flops=None):
    out = [jax.ShapeDtypeStruct(shape, F32) for shape in shapes]
    cost = None
    if flops is not None:
        cost = pl.CostEstimate(flops=flops, bytes_accessed=0, transcendentals=0)
    return pl.pallas_call(
        kernel,
        out_shape=out,
        in_specs=[pl.BlockSpec(memory_space=where)] * len(operands),
        out_specs=[pl.BlockSpec(memory_space=pltpu.VMEM)] * len(out),
        scratch_shapes=scratch,
        cost_estimate=cost,
        compiler_params=pltpu.CompilerParams(vmem_limit_bytes=32 * 1024 * 1024),
    )(*operands)


def on_each_component(atmosphere, ocean):
    comp = lax.axis_index("comp")
    pl.when(comp == 0)(atmosphere)
    pl.when(comp != 0)(ocean)


def fold(source, target, first, halves):
    width = halves.shape[1]
    rows = halves.shape[0]
    lines = rows // SPAN
    for h in range(target.shape[1] // width):
        for j in range(lines):
            at = j * target.shape[1] + h * width
            halves[pl.ds(j, SPAN, stride=lines), :] = source[:, at : at + width].astype(F32)
        target[first : first + rows, h * width : h * width + width] = halves[...]


def gather_steps(table, index, out):
    rows, width = index.shape
    tiles = [(r, h) for r in range(0, rows, 8) for h in range(0, width, 128)]
    pieces = [index[r : r + 8, h : h + 128] for r, h in tiles]
    high = [lax.shift_right_logical(p, 7) for p in pieces]
    low = [p & 127 for p in pieces]
    found = [jnp.zeros((8, 128), F32) for _ in tiles]
    for i in range(rows * width // 128):
        r, h = divmod(i * 128, width)
        line = jnp.broadcast_to(table[r : r + 1, h : h + 128], (8, 128))
        for k in range(len(tiles)):
            picked = jnp.take_along_axis(line, low[k], axis=1, mode="promise_in_bounds")
            found[k] = jnp.where(high[k] == i, picked, found[k])
        yield
    across = width // 128
    lines = [jnp.concatenate(found[k : k + across], 1) for k in range(0, len(found), across)]
    out.append(jnp.concatenate(lines, 0))


def scatter_steps(totals, values, index):
    rows, width = index.shape
    place = lax.broadcasted_iota(I32, (64, width), 0)
    for r in range(rows):
        cell = index[r : r + 1, :]
        value = values[r : r + 1, :]
        head = value.astype(BF16).astype(F32)
        tail = value - head
        row_here = place == lax.shift_right_logical(cell, 6)
        column_here = place == (cell & 63)
        spread = jnp.concatenate(
            [
                jnp.where(row_here, head, 0.0).astype(BF16),
                jnp.where(row_here, tail, 0.0).astype(BF16),
            ],
            0,
        )
        chosen = jnp.where(column_here, 1.0, 0.0).astype(BF16)
        totals.append(
            totals.pop()
            + lax.dot_general(spread, chosen, CONTRACT_LANES, preferred_element_type=F32)
        )
        yield


def remap(parts):
    totals = [jnp.zeros((128, 64), F32)]
    adding = iter(())
    for table, cells, weights, targets in parts:
        found = []
        for step, _ in enumerate(gather_steps(table, cells, found)):
            if step % 2:
                next(adding, None)
        for _ in adding:
            pass
        adding = scatter_steps(totals, weights * found[0], targets)
    for _ in adding:
        pass
    return as_rows(totals[0])


def scatter_add(total, values, index):
    totals = [total]
    for _ in scatter_steps(totals, values, index):
        pass
    return totals[0]


def as_rows(total):
    both = total[:64] + total[64:]
    cells = both.reshape(16, 4, 64)
    return jnp.concatenate([cells[:, q, :] for q in range(4)], 1)


def pack_kernel(cells, weights, slots, state, coeff, vertical, pack, code, ints, reals, codes, halves, sems):
    copies = [
        pltpu.make_async_copy(state.at[0], pack.at[256:272], sems.at[0]),
        pltpu.make_async_copy(coeff.at[0], pack.at[272:288], sems.at[1]),
        pltpu.make_async_copy(vertical, codes, sems.at[2]),
    ]
    for copy in copies:
        copy.start()

    def atmosphere():
        first = pltpu.make_async_copy(cells, ints, sems.at[3])
        second = pltpu.make_async_copy(weights, reals, sems.at[4])
        first.start()
        second.start()
        first.wait()
        fold(ints, pack, 0, halves)
        second.wait()
        fold(reals, pack, 128, halves)

    def ocean():
        first = pltpu.make_async_copy(slots, ints, sems.at[3])
        first.start()
        pack[128:256, :] = jnp.zeros((128, pack.shape[1]), F32)
        first.wait()
        ints[...] = renumbered(ints[...])
        fold(ints, pack, 0, halves)

    on_each_component(atmosphere, ocean)
    for copy in copies:
        copy.wait()
    code[...] = halved(codes[...].astype(F32))

    @pl.when(lax.axis_index("comp") != 0)
    def _():
        pack[256:272, :] = halved(pack[256:272, :])
        pack[272:288, :] = halved(pack[272:288, :])


def halved(x):
    width = x.shape[1] // 2
    a, b = x[:, :width], x[:, width:]
    lane = lax.broadcasted_iota(I32, a.shape, 1)

    def picked(odd):
        index = ((2 * lane) & (width - 1)) + odd
        first = jnp.take_along_axis(a, index, axis=1, mode="promise_in_bounds")
        second = jnp.take_along_axis(b, index, axis=1, mode="promise_in_bounds")
        return jnp.where(lane < width // 2, first, second)

    return jnp.concatenate([picked(0), picked(1)], 1)


def unhalved(a, b):
    lane = lax.broadcasted_iota(I32, a.shape, 1)
    width = a.shape[1]

    def picked(first):
        index = lax.shift_right_logical(lane, 1) + first
        even = jnp.take_along_axis(a, index, axis=1, mode="promise_in_bounds")
        odd = jnp.take_along_axis(b, index, axis=1, mode="promise_in_bounds")
        return jnp.where((lane & 1) == 0, even, odd)

    return jnp.concatenate([picked(0), picked(width // 2)], 1)


def renumbered(cell):
    return (cell & ~255) + lax.shift_left(cell & 1, 7) + lax.shift_right_logical(cell & 255, 1)


def block_of(ref, k):
    return ref[16 * k : 16 * k + 16]


def message_kernel(pack, other, code, m1, m2, m3, m4, edge):
    def fill(air, sea, rows, rows_back):
        s = air[256:272, :]
        coeff = air[272:288, :]
        none = jnp.zeros_like(s[0:1])
        near = jnp.concatenate([none, s[:-1]], 0) + jnp.concatenate([s[1:], none], 0)
        near = near + pltpu.roll(s, 1, 1) + pltpu.roll(s, s.shape[1] - 1, 1)
        flux = coeff * (s + 0.2 * (near - 4.0 * s))
        ends = jnp.concatenate([coeff[0:1], coeff[15:16], s[0:1], s[15:16], none, none, none, none], 0)
        for j, m in enumerate((m1, m2, m3)):
            m[0:16, :] = block_of(air, rows[j])
            m[16:32, :] = block_of(air, 8 + rows[j])
            m[32:48, :] = flux
            m[48:64, :] = block_of(sea, rows_back[j])
            m[64:72, :] = ends
            m[72:88, :] = sea[272:288, :]
            m[88:104, :] = code[...]
            m[104:120, :] = sea[256:272, :]
        m4[32:48, :] = flux
        m4[48:56, :] = ends
        m4[56:72, :] = sea[272:288, :]
        m4[72:88, :] = code[...]
        edge[...] = s[0:8]

    def atmosphere():
        fill(pack, other, (3, 2, 1), (5, 6, 7))
        m4[0:16, :] = block_of(pack, 0)
        m4[16:32, :] = block_of(pack, 8)

    def ocean():
        fill(other, pack, (5, 6, 7), (3, 2, 1))
        m4[0:16, :] = block_of(pack, 0)
        m4[16:32, :] = pack[256:272, :]

    on_each_component(atmosphere, ocean)


def share_kernel(pack, inverse):
    def atmosphere():
        total = jnp.zeros((128, 64), F32)
        for d in range(SPAN):
            total = scatter_add(total, block_of(pack, 8 + d), block_of(pack, d).astype(I32))
        inverse[...] = 1.0 / as_rows(total)

    def ocean():
        inverse[...] = jnp.ones_like(inverse)

    on_each_component(atmosphere, ocean)


def edge_kernel(edge, out):
    out[...] = edge[...]


def whole_flux(flux, ends, before, after):
    first = flux[0:1] + ends[0:1] * (0.2 * before)
    last = flux[15:16] + ends[1:2] * (0.2 * after)
    return jnp.concatenate([first, flux[1:15], last], 0)


def flux_kernel(edge, m1, m2, m3, m4, own, pack, other, partial):
    atmosphere = lax.axis_index("comp") == 0

    def either(a, b):
        return jnp.where(atmosphere, a, b)

    def part(cells, weights, flux, ends, before, after, slots):
        return whole_flux(flux, ends, before, after), cells.astype(I32), weights, slots.astype(I32)

    def sent(m):
        return m[0:16, :], m[16:32, :], m[32:48, :], m[64:72, :]

    parts = []
    before = either(pack[271:272, :], m2[67:68, :])
    after = either(m2[66:67, :], other[256:257, :])
    parts.append(part(*sent(m1), before, after, either(block_of(other, 3), block_of(pack, 5))))
    before = either(m1[67:68, :], m3[67:68, :])
    after = either(m3[66:67, :], m1[66:67, :])
    parts.append(part(*sent(m2), before, after, either(block_of(other, 2), block_of(pack, 6))))
    before = either(m2[67:68, :], m4[51:52, :])
    after = either(m4[50:51, :], m2[66:67, :])
    parts.append(part(*sent(m3), before, after, either(block_of(other, 1), block_of(pack, 7))))
    before = either(m3[67:68, :], m1[67:68, :])
    cells = either(m4[0:16, :], block_of(other, 4))
    weights = either(m4[16:32, :], block_of(other, 12))
    flux = either(m4[32:48, :], own[32:48, :])
    ends = either(m4[48:56, :], own[64:72, :])
    slots = either(block_of(other, 0), block_of(pack, 4))
    parts.append(part(cells, weights, flux, ends, before, edge[0:1, :], slots))
    partial[...] = remap(parts)


def source_kernel(partial, partial_sw, pack, other, code, rhs, fifth, sixth):
    atmosphere = lax.axis_index("comp") == 0
    sea = jnp.where(atmosphere, other[256:272, :], pack[256:272, :])
    diagonal = jnp.where(atmosphere, other[272:288, :], pack[272:288, :])
    total = partial[...] + partial_sw[...] + sea
    rhs[...] = total
    for k, part in enumerate((total, diagonal, code[...])):
        fifth[16 * k : 16 * k + 16, :] = part
        sixth[8 * k : 8 * k + 8, :] = part[8:16]


def near_kernel(p1, p2, m1, m2, out):
    out[0:16, :] = p1[...]
    out[16:48, :] = m1[72:104, :]
    out[48:56, :] = p2[8:16, :]
    out[56:64, :] = m2[80:88, :]
    out[64:72, :] = m2[96:104, :]


def trace_kernel(
    pack, other, inverse, own, near, fifth, sixth, p1, p2, p3, p4, m1, m2, m3, m4,
    send, keep, rhs, inv, code, code_up, code_down, even, odd,
):
    rows, width = rhs.shape
    groups = rows // 8

    def place(parts):
        at = 0
        for right, diagonal, face in parts:
            size = right.shape[0]
            rhs[at : at + size, :] = right[...]
            inv[at : at + size, :] = 1.0 / (diagonal[...] + 3.0)
            code[at : at + size, :] = face[...]
            at += size

    def thirds(ref, first, step, size):
        return [ref.at[first + k * step : first + k * step + size] for k in range(3)]

    others = [(p, m.at[72:88], m.at[88:104]) for p, m in ((p1, m1), (p2, m2), (p3, m3))]
    others.append((p4, m4.at[56:72], m4.at[72:88]))
    here = thirds(own, 0, 16, 16)
    on_each_component(
        lambda: place(
            [thirds(near, 48, 8, 8), thirds(near, 0, 16, 16), here, *others, thirds(fifth, 0, 16, 8)]
        ),
        lambda: place(
            [thirds(sixth, 0, 8, 8), thirds(fifth, 0, 16, 16), *others[::-1], here, thirds(near, 0, 16, 8)]
        ),
    )
    line = lax.broadcasted_iota(I32, (8, width), 0)

    def group(ref, g):
        return ref[8 * g : 8 * g + 8, :]

    def from_above(here, above):
        return jnp.where(line[:, : here.shape[1]] == 0, above, here)

    def from_below(here, below):
        return jnp.where(line[:, : here.shape[1]] == 7, below, here)

    downward = [pltpu.roll(group(code, g), 1, 0) for g in range(groups)]
    for g in range(groups):
        code_down[8 * g : 8 * g + 8, :] = from_above(downward[g], downward[max(g - 1, 0)])
    upward = [pltpu.roll(group(code, g), 7, 0) for g in range(groups)]
    for g in range(groups):
        code_up[8 * g : 8 * g + 8, :] = from_below(upward[g], upward[min(g + 1, groups - 1)])
    half = width // 2
    for g in range(groups):
        first = group(rhs, g) * group(inv, g)
        even[8 * g : 8 * g + 8, :] = first[:, :half]
        odd[8 * g : 8 * g + 8, :] = first[:, half:]

    def sweep(first, last):
        beside, above, below = {}, {}, {}

        def chosen(code, zero, left, here, right):
            return jnp.where(code == zero, left, jnp.where(code == zero + 1.0, here, right))

        def read(g):
            e, o = group(even, g), group(odd, g)
            left = pltpu.roll(o, 1, 1)
            right = pltpu.roll(e, half - 1, 1)
            beside[g] = left + o, e + right
            u, d = group(code_up, g), group(code_down, g)
            up = (chosen(u[:, :half], 0.0, left, e, o), chosen(u[:, half:], 0.0, e, o, right))
            down = (chosen(d[:, :half], 3.0, left, e, o), chosen(d[:, half:], 3.0, e, o, right))
            above[g] = [pltpu.roll(x, 1, 0) for x in up]
            below[g] = [pltpu.roll(x, 7, 0) for x in down]

        def write(g):
            for k, ref in enumerate((even, odd)):
                lanes = slice(k * half, k * half + half)
                up = from_above(above[g][k], above[max(g - 1, first)][k])
                down = from_below(below[g][k], below[min(g + 1, last - 1)][k])
                third = jnp.where(group(code, g)[:, lanes] >= 3.0, down, up)
                total = group(rhs, g)[:, lanes] + (beside[g][k] + third)
                ref[8 * g : 8 * g + 8, :] = total * group(inv, g)[:, lanes]

        for g in range(first, last):
            read(g)
            if g > first:
                write(g - 1)
        write(last - 1)

    def repeat(count, skip):
        def several(_, carry):
            for _ in range(8):
                sweep(skip, groups - skip)
            return carry

        for _ in range(count % 8):
            sweep(skip, groups - skip)
        if count >= 8:
            lax.fori_loop(0, count // 8, several, 0)

    done = 1
    for skip in range(3):
        until = min(SWEEPS, SWEEPS - 16 + 8 * skip)
        repeat(until - done, skip)
        done = until

    atmosphere = lax.axis_index("comp") == 0
    states = [m[104:120, :] for m in (m1, m2, m3)]
    sea = [jnp.where(atmosphere, other[256:272, :], m4[16:32, :])]
    sea += [jnp.where(atmosphere, states[i], states[2 - i]) for i in range(3)]
    slots = [jnp.where(atmosphere, block_of(other, 4), m4[0:16, :])]
    for a, b in ((m1, m3), (m2, m2), (m3, m1)):
        slots.append(jnp.where(atmosphere, a[48:64, :], b[48:64, :]))
    parts = []
    for i in range(4):
        at = 24 + 16 * i
        eta = jnp.concatenate([even[at : at + 16, :], odd[at : at + 16, :]], 1)
        sst = 1.25 * sea[i] + 0.5 * eta - 0.25 * rhs[at : at + 16, :]
        cell = jnp.where(atmosphere, block_of(pack, 4 + i), block_of(other, i)).astype(I32)
        weight = jnp.where(atmosphere, block_of(pack, 12 + i), block_of(other, 8 + i))
        parts.append((sst, slots[i].astype(I32), weight, cell))
    part = remap(parts)
    send[...] = jnp.where(atmosphere, unhalved(even[24:40, :], odd[24:40, :]), part)
    keep[...] = jnp.where(atmosphere, part * inverse[...], 0.0)


def shards(state, coeff, vertical, send_cell, incoming_marine_slot, remap_weight):
    tiles = lax.axis_size("tile")
    block = state.shape[1:]
    lines, width = block

    def swap(x):
        return lax.ppermute(x, "comp", [(0, 1), (1, 0)])

    def move(x, atmosphere_from, ocean_from):
        pairs = [((t + atmosphere_from) % tiles, t) for t in range(tiles)]
        pairs += [(tiles + (t + ocean_from) % tiles, tiles + t) for t in range(tiles)]
        return lax.ppermute(x, GRID, pairs)

    arguments = (send_cell, remap_weight, incoming_marine_slot, state, coeff, vertical)
    pack, code = call(
        pack_kernel, [(18 * lines, width), block],
        *[pltpu.with_memory_space_constraint(x, pltpu.HBM) for x in arguments],
        scratch=[
            pltpu.VMEM(send_cell.shape, I32),
            pltpu.VMEM(send_cell.shape, F32),
            pltpu.VMEM(block, I32),
            pltpu.VMEM((SPAN * lines, 128), F32),
            pltpu.SemaphoreType.DMA((5,)),
        ],
        where=pltpu.HBM,
    )
    other = swap(pack)
    tall = 4 * lines + 8
    *messages, edge = call(
        message_kernel,
        [(tall + 3 * lines, width)] * 3 + [(tall + lines, width), (8, width)],
        pack, other, code,
    )
    (edge_in,) = call(edge_kernel, [(8, width)], move(edge, 5, 1), flops=10**9)
    m1_in, m2_in, m3_in, m4_in = messages_in = [move(m, j, -j) for j, m in enumerate(messages, 1)]
    (inverse,) = call(share_kernel, [block], pack, flops=10**9)
    (partial,) = call(flux_kernel, [block], edge_in, *messages_in, messages[1], pack, other, flops=10**9)
    rhs, fifth, sixth = call(
        source_kernel, [block, (3 * lines, width), (24, width)], partial, swap(partial), pack, other, code
    )
    p1_in, p2_in, p3_in, p4_in = (move(rhs, j, -j) for j in range(1, 5))
    fifth_in = move(fifth, 5, -5)
    sixth_in = lax.ppermute(sixth, GRID, [(tiles + t, tiles + (t + 6) % tiles) for t in range(tiles)])
    (near,) = call(near_kernel, [(72, width)], p1_in, p2_in, m1_in, m2_in)
    window = (6 * lines + 16, width)
    send, keep = call(
        trace_kernel, [block, block],
        pack, other, inverse, fifth, swap(near), fifth_in, sixth_in, p1_in, p2_in, p3_in, p4_in, *messages_in,
        scratch=[pltpu.VMEM(window, F32)] * 5
        + [pltpu.VMEM((window[0], width // 2), F32)] * 2,
    )
    return (keep + swap(send) * inverse)[None]


def solution(mesh):
    table = P(GRID, None)
    grid = P("comp", "tile", None)
    return jax.shard_map(
        shards,
        mesh=mesh,
        in_specs=(grid, grid, P("tile", None), table, table, table),
        out_specs=grid,
        check_vma=False,
    )
```

```python
import jax
import jax.experimental.pallas as pl
import jax.experimental.pallas.tpu as pltpu
import jax.numpy as jnp
from jax import lax
from jax.sharding import PartitionSpec as P

SPAN = 8
SWEEPS = 20
MIDDLE = SPAN // 2
F32 = jnp.float32
BF16 = jnp.bfloat16
I32 = jnp.int32
CONTRACT_LANES = (((1,), (1,)), ((), ()))
GRID = ("comp", "tile")


def call(kernel, shapes, *operands, scratch=(), where=pltpu.VMEM, flops=None):
    out = [jax.ShapeDtypeStruct(shape, F32) for shape in shapes]
    cost = None
    if flops is not None:
        cost = pl.CostEstimate(flops=flops, bytes_accessed=0, transcendentals=0)
    return pl.pallas_call(
        kernel,
        out_shape=out,
        in_specs=[pl.BlockSpec(memory_space=where)] * len(operands),
        out_specs=[pl.BlockSpec(memory_space=pltpu.VMEM)] * len(out),
        scratch_shapes=scratch,
        cost_estimate=cost,
        compiler_params=pltpu.CompilerParams(vmem_limit_bytes=32 * 1024 * 1024),
    )(*operands)


def on_each_component(atmosphere, ocean):
    comp = lax.axis_index("comp")
    pl.when(comp == 0)(atmosphere)
    pl.when(comp != 0)(ocean)


def fold(source, target, first, halves):
    width = halves.shape[1]
    rows = halves.shape[0]
    lines = rows // SPAN
    for h in range(target.shape[1] // width):
        for j in range(lines):
            at = j * target.shape[1] + h * width
            halves[pl.ds(j, SPAN, stride=lines), :] = source[:, at : at + width].astype(F32)
        target[first : first + rows, h * width : h * width + width] = halves[...]


def gather_steps(table, index, out):
    rows, width = index.shape
    tiles = [(r, h) for r in range(0, rows, 8) for h in range(0, width, 128)]
    pieces = [index[r : r + 8, h : h + 128] for r, h in tiles]
    high = [lax.shift_right_logical(p, 7) for p in pieces]
    low = [p & 127 for p in pieces]
    found = [jnp.zeros((8, 128), F32) for _ in tiles]
    for i in range(rows * width // 128):
        r, h = divmod(i * 128, width)
        line = jnp.broadcast_to(table[r : r + 1, h : h + 128], (8, 128))
        for k in range(len(tiles)):
            picked = jnp.take_along_axis(line, low[k], axis=1, mode="promise_in_bounds")
            found[k] = jnp.where(high[k] == i, picked, found[k])
        yield
    across = width // 128
    lines = [jnp.concatenate(found[k : k + across], 1) for k in range(0, len(found), across)]
    out.append(jnp.concatenate(lines, 0))


def scatter_steps(totals, values, index):
    rows, width = index.shape
    place = lax.broadcasted_iota(I32, (64, width), 0)
    for r in range(rows):
        cell = index[r : r + 1, :]
        value = values[r : r + 1, :]
        head = value.astype(BF16).astype(F32)
        tail = value - head
        row_here = place == lax.shift_right_logical(cell, 6)
        column_here = place == (cell & 63)
        spread = jnp.concatenate(
            [
                jnp.where(row_here, head, 0.0).astype(BF16),
                jnp.where(row_here, tail, 0.0).astype(BF16),
            ],
            0,
        )
        chosen = jnp.where(column_here, 1.0, 0.0).astype(BF16)
        totals.append(
            totals.pop()
            + lax.dot_general(spread, chosen, CONTRACT_LANES, preferred_element_type=F32)
        )
        yield


def remap(parts, total):
    totals = [total]
    adding = iter(())
    for table, cells, weights, targets in parts:
        found = []
        for step, _ in enumerate(gather_steps(table, cells, found)):
            if step % 2:
                next(adding, None)
        for _ in adding:
            pass
        adding = scatter_steps(totals, weights * found[0], targets)
    for _ in adding:
        pass
    return totals[0]


def scatter_add(total, values, index):
    totals = [total]
    for _ in scatter_steps(totals, values, index):
        pass
    return totals[0]


def as_rows(total):
    both = total[:64] + total[64:]
    cells = both.reshape(16, 4, 64)
    return jnp.concatenate([cells[:, q, :] for q in range(4)], 1)


def pack_kernel(cells, weights, slots, state, coeff, vertical, pack, code, ints, reals, codes, halves, sems):
    copies = [
        pltpu.make_async_copy(state.at[0], pack.at[256:272], sems.at[0]),
        pltpu.make_async_copy(coeff.at[0], pack.at[272:288], sems.at[1]),
        pltpu.make_async_copy(vertical, codes, sems.at[2]),
    ]
    for copy in copies:
        copy.start()

    def atmosphere():
        first = pltpu.make_async_copy(cells, ints, sems.at[3])
        second = pltpu.make_async_copy(weights, reals, sems.at[4])
        first.start()
        second.start()
        first.wait()
        fold(ints, pack, 0, halves)
        second.wait()
        fold(reals, pack, 128, halves)

    def ocean():
        first = pltpu.make_async_copy(slots, ints, sems.at[3])
        first.start()
        pack[128:256, :] = jnp.zeros((128, pack.shape[1]), F32)
        first.wait()
        ints[...] = renumbered(ints[...])
        fold(ints, pack, 0, halves)

    on_each_component(atmosphere, ocean)
    for copy in copies:
        copy.wait()
    code[...] = halved(codes[...].astype(F32))

    @pl.when(lax.axis_index("comp") != 0)
    def _():
        pack[256:272, :] = halved(pack[256:272, :])
        pack[272:288, :] = halved(pack[272:288, :])


def halved(x):
    width = x.shape[1] // 2
    a, b = x[:, :width], x[:, width:]
    lane = lax.broadcasted_iota(I32, a.shape, 1)

    def picked(odd):
        index = ((2 * lane) & (width - 1)) + odd
        first = jnp.take_along_axis(a, index, axis=1, mode="promise_in_bounds")
        second = jnp.take_along_axis(b, index, axis=1, mode="promise_in_bounds")
        return jnp.where(lane < width // 2, first, second)

    return jnp.concatenate([picked(0), picked(1)], 1)


def unhalved(a, b):
    lane = lax.broadcasted_iota(I32, a.shape, 1)
    width = a.shape[1]

    def picked(first):
        index = lax.shift_right_logical(lane, 1) + first
        even = jnp.take_along_axis(a, index, axis=1, mode="promise_in_bounds")
        odd = jnp.take_along_axis(b, index, axis=1, mode="promise_in_bounds")
        return jnp.where((lane & 1) == 0, even, odd)

    return jnp.concatenate([picked(0), picked(width // 2)], 1)


def renumbered(cell):
    return (cell & ~255) + lax.shift_left(cell & 1, 7) + lax.shift_right_logical(cell & 255, 1)


def block_of(ref, k):
    return ref[16 * k : 16 * k + 16]


def message_kernel(pack, other, code, m1, m2, m3, m4, edge):
    def fill(air, sea, rows, rows_back):
        s = air[256:272, :]
        coeff = air[272:288, :]
        none = jnp.zeros_like(s[0:1])
        near = jnp.concatenate([none, s[:-1]], 0) + jnp.concatenate([s[1:], none], 0)
        near = near + pltpu.roll(s, 1, 1) + pltpu.roll(s, s.shape[1] - 1, 1)
        flux = coeff * (s + 0.2 * (near - 4.0 * s))
        ends = jnp.concatenate([coeff[0:1], coeff[15:16], s[0:1], s[15:16], none, none, none, none], 0)
        for j, m in enumerate((m1, m2, m3)):
            m[0:16, :] = block_of(air, rows[j])
            m[16:32, :] = block_of(air, 8 + rows[j])
            m[32:48, :] = flux
            m[48:64, :] = block_of(sea, rows_back[j])
            m[64:72, :] = ends
            m[72:88, :] = sea[272:288, :]
            m[88:104, :] = code[...]
            m[104:120, :] = sea[256:272, :]
        m4[32:48, :] = flux
        m4[48:56, :] = ends
        m4[56:72, :] = sea[272:288, :]
        m4[72:88, :] = code[...]
        edge[...] = s[0:8]

    def atmosphere():
        fill(pack, other, (3, 2, 1), (5, 6, 7))
        m4[0:16, :] = block_of(pack, 0)
        m4[16:32, :] = block_of(pack, 8)

    def ocean():
        fill(other, pack, (5, 6, 7), (3, 2, 1))
        m4[0:16, :] = block_of(pack, 0)
        m4[16:32, :] = pack[256:272, :]

    on_each_component(atmosphere, ocean)


def share_kernel(pack, other, share):
    def fill(air, first):
        total = jnp.zeros((128, 64), F32)
        for d in range(first, first + SPAN // 2):
            total = scatter_add(total, block_of(air, 8 + d), block_of(air, d).astype(I32))
        share[...] = as_rows(total)

    on_each_component(lambda: fill(pack, 4), lambda: fill(other, 0))


def edge_kernel(edge, total, out, same):
    out[...] = edge[...]
    same[...] = total[...]


def whole_flux(flux, ends, before, after):
    first = flux[0:1] + ends[0:1] * (0.2 * before)
    last = flux[15:16] + ends[1:2] * (0.2 * after)
    return jnp.concatenate([first, flux[1:15], last], 0)


def flux_part(cells, weights, flux, ends, before, after, slots):
    return whole_flux(flux, ends, before, after), cells.astype(I32), weights, slots.astype(I32)


def sent(m):
    return m[0:16, :], m[16:32, :], m[32:48, :], m[64:72, :]


def first_flux_kernel(m1, m2, m3, pack, other, total):
    atmosphere = lax.axis_index("comp") == 0

    def either(a, b):
        return jnp.where(atmosphere, a, b)

    parts = []
    before = either(pack[271:272, :], m2[67:68, :])
    after = either(m2[66:67, :], other[256:257, :])
    parts.append(flux_part(*sent(m1), before, after, either(block_of(other, 3), block_of(pack, 5))))
    before = either(m1[67:68, :], m3[67:68, :])
    after = either(m3[66:67, :], m1[66:67, :])
    parts.append(flux_part(*sent(m2), before, after, either(block_of(other, 2), block_of(pack, 6))))
    total[...] = remap(parts, jnp.zeros((128, 64), F32))


def second_flux_kernel(edge, m4, m1, m2, m3, own, pack, other, total, partial):
    atmosphere = lax.axis_index("comp") == 0

    def either(a, b):
        return jnp.where(atmosphere, a, b)

    parts = []
    before = either(m3[67:68, :], m1[67:68, :])
    cells = either(m4[0:16, :], block_of(other, 4))
    weights = either(m4[16:32, :], block_of(other, 12))
    flux = either(m4[32:48, :], own[32:48, :])
    ends = either(m4[48:56, :], own[64:72, :])
    slots = either(block_of(other, 0), block_of(pack, 4))
    parts.append(flux_part(cells, weights, flux, ends, before, edge[0:1, :], slots))
    before = either(m2[67:68, :], m4[51:52, :])
    after = either(m4[50:51, :], m2[66:67, :])
    parts.append(flux_part(*sent(m3), before, after, either(block_of(other, 1), block_of(pack, 7))))
    partial[...] = as_rows(remap(parts, total[...]))


def source_kernel(partial, partial_sw, pack, other, code, m4, rhs, first, second, sixth):
    atmosphere = lax.axis_index("comp") == 0
    sea = jnp.where(atmosphere, other[256:272, :], pack[256:272, :])
    total = partial[...] + partial_sw[...] + sea
    rhs[...] = total
    first[0:16, :] = total
    first[16:48, :] = m4[56:88, :]
    second[0:16, :] = total
    second[16:24, :] = m4[64:72, :]
    second[24:32, :] = m4[80:88, :]
    sixth[...] = total[8:16]


def near_kernel(p1, p2, m1, m2, out):
    out[0:16, :] = p1[0:16, :]
    out[16:48, :] = m1[72:104, :]
    out[48:56, :] = p2[8:16, :]
    out[56:64, :] = m2[80:88, :]
    out[64:72, :] = m2[96:104, :]


def trace_kernel(
    pack, other, share, code_own, own, near, fifth, sixth, p1, p2, p3, p4, m1, m2, m3, m4,
    send, keep, rhs, inv, code, code_up, code_down, even, odd,
):
    rows, width = rhs.shape
    groups = rows // 8

    def place(parts):
        at = 0
        for right, diagonal, face in parts:
            size = right.shape[0]
            rhs[at : at + size, :] = right[...]
            inv[at : at + size, :] = 1.0 / (diagonal[...] + 3.0)
            code[at : at + size, :] = face[...]
            at += size

    def thirds(ref, first, step, size):
        return [ref.at[first + k * step : first + k * step + size] for k in range(3)]

    others = [(p.at[0:16], m.at[72:88], m.at[88:104]) for p, m in ((p1, m1), (p2, m2), (p3, m3))]
    others.append((p4, m4.at[56:72], m4.at[72:88]))
    further = p1.at[16:24], p1.at[32:40]
    whole = p1.at[16:32], p1.at[32:48]
    last = p2.at[16:24], p2.at[24:32]
    on_each_component(
        lambda: place(
            [thirds(near, 48, 8, 8), thirds(near, 0, 16, 16), (own, other.at[272:288], code_own), *others,
             (fifth.at[0:8], *further)]
        ),
        lambda: place(
            [(sixth, *last), (fifth, *whole), *others[::-1], (own, pack.at[272:288], code_own),
             thirds(near, 0, 16, 8)]
        ),
    )
    line = lax.broadcasted_iota(I32, (8, width), 0)

    def group(ref, g):
        return ref[8 * g : 8 * g + 8, :]

    def from_above(here, above):
        return jnp.where(line[:, : here.shape[1]] == 0, above, here)

    def from_below(here, below):
        return jnp.where(line[:, : here.shape[1]] == 7, below, here)

    downward = [pltpu.roll(group(code, g), 1, 0) for g in range(groups)]
    for g in range(groups):
        code_down[8 * g : 8 * g + 8, :] = from_above(downward[g], downward[max(g - 1, 0)])
    upward = [pltpu.roll(group(code, g), 7, 0) for g in range(groups)]
    for g in range(groups):
        code_up[8 * g : 8 * g + 8, :] = from_below(upward[g], upward[min(g + 1, groups - 1)])
    half = width // 2
    for g in range(groups):
        first = group(rhs, g) * group(inv, g)
        even[8 * g : 8 * g + 8, :] = first[:, :half]
        odd[8 * g : 8 * g + 8, :] = first[:, half:]

    def sweep(first, last):
        beside, above, below = {}, {}, {}

        def chosen(code, zero, left, here, right):
            return jnp.where(code == zero, left, jnp.where(code == zero + 1.0, here, right))

        def read(g):
            e, o = group(even, g), group(odd, g)
            left = pltpu.roll(o, 1, 1)
            right = pltpu.roll(e, half - 1, 1)
            beside[g] = left + o, e + right
            u, d = group(code_up, g), group(code_down, g)
            up = (chosen(u[:, :half], 0.0, left, e, o), chosen(u[:, half:], 0.0, e, o, right))
            down = (chosen(d[:, :half], 3.0, left, e, o), chosen(d[:, half:], 3.0, e, o, right))
            above[g] = [pltpu.roll(x, 1, 0) for x in up]
            below[g] = [pltpu.roll(x, 7, 0) for x in down]

        def write(g):
            for k, ref in enumerate((even, odd)):
                lanes = slice(k * half, k * half + half)
                up = from_above(above[g][k], above[max(g - 1, first)][k])
                down = from_below(below[g][k], below[min(g + 1, last - 1)][k])
                third = jnp.where(group(code, g)[:, lanes] >= 3.0, down, up)
                total = group(rhs, g)[:, lanes] + (beside[g][k] + third)
                ref[8 * g : 8 * g + 8, :] = total * group(inv, g)[:, lanes]

        for g in range(first, last):
            read(g)
            if g > first:
                write(g - 1)
        write(last - 1)

    def repeat(count, skip):
        def several(_, carry):
            for _ in range(8):
                sweep(skip, groups - skip)
            return carry

        for _ in range(count % 8):
            sweep(skip, groups - skip)
        if count >= 8:
            lax.fori_loop(0, count // 8, several, 0)

    done = 1
    for skip in range(3):
        until = min(SWEEPS, SWEEPS - 16 + 8 * skip)
        repeat(until - done, skip)
        done = until

    atmosphere = lax.axis_index("comp") == 0
    states = [m[104:120, :] for m in (m1, m2, m3)]
    sea = [jnp.where(atmosphere, other[256:272, :], m4[16:32, :])]
    sea += [jnp.where(atmosphere, states[i], states[2 - i]) for i in range(3)]
    slots = [jnp.where(atmosphere, block_of(other, 4), m4[0:16, :])]
    for a, b in ((m1, m3), (m2, m2), (m3, m1)):
        slots.append(jnp.where(atmosphere, a[48:64, :], b[48:64, :]))
    parts = []
    for i in range(4):
        at = 24 + 16 * i
        eta = jnp.concatenate([even[at : at + 16, :], odd[at : at + 16, :]], 1)
        sst = 1.25 * sea[i] + 0.5 * eta - 0.25 * rhs[at : at + 16, :]
        cell = jnp.where(atmosphere, block_of(pack, 4 + i), block_of(other, i)).astype(I32)
        weight = jnp.where(atmosphere, block_of(pack, 12 + i), block_of(other, 8 + i))
        parts.append((sst, slots[i].astype(I32), weight, cell))
    part = as_rows(remap(parts, jnp.zeros((128, 64), F32)))
    send[0:16, :] = jnp.where(atmosphere, unhalved(even[24:40, :], odd[24:40, :]), part)
    send[16:32, :] = jnp.where(atmosphere, 1.0, share[...])
    keep[0:16, :] = jnp.where(atmosphere, part, 0.0)
    keep[16:32, :] = jnp.where(atmosphere, share[...], 0.0)


def shards(state, coeff, vertical, send_cell, incoming_marine_slot, remap_weight):
    tiles = lax.axis_size("tile")
    block = state.shape[1:]
    lines, width = block

    def swap(x):
        return lax.ppermute(x, "comp", [(0, 1), (1, 0)])

    def move(x, atmosphere_from, ocean_from):
        pairs = [((t + atmosphere_from) % tiles, t) for t in range(tiles)]
        pairs += [(tiles + (t + ocean_from) % tiles, tiles + t) for t in range(tiles)]
        return lax.ppermute(x, GRID, pairs)

    arguments = (send_cell, remap_weight, incoming_marine_slot, state, coeff, vertical)
    pack, code = call(
        pack_kernel, [(18 * lines, width), block],
        *[pltpu.with_memory_space_constraint(x, pltpu.HBM) for x in arguments],
        scratch=[
            pltpu.VMEM(send_cell.shape, I32),
            pltpu.VMEM(send_cell.shape, F32),
            pltpu.VMEM(block, I32),
            pltpu.VMEM((SPAN * lines, 128), F32),
            pltpu.SemaphoreType.DMA((5,)),
        ],
        where=pltpu.HBM,
    )
    other = swap(pack)
    tall = 4 * lines + 8
    *messages, edge = call(
        message_kernel,
        [(tall + 3 * lines, width)] * 3 + [(tall + lines, width), (8, width)],
        pack, other, code,
    )
    edge_in = move(edge, 5, 1)
    m1_in, m2_in, m3_in, m4_in = messages_in = [move(m, j, -j) for j, m in enumerate(messages, 1)]
    (share,) = call(share_kernel, [block], pack, other, flops=10**9)
    (total,) = call(first_flux_kernel, [(128, 64)], m1_in, m2_in, m3_in, pack, other, flops=None)
    edge_in, total = call(edge_kernel, [(8, width), (128, 64)], edge_in, total, flops=10**8)
    (partial,) = call(
        second_flux_kernel, [block],
        edge_in, m4_in, m1_in, m2_in, m3_in, messages[1], pack, other, total, flops=10**9,
    )
    rhs, first, second, sixth = call(
        source_kernel,
        [block, (3 * lines, width), (2 * lines, width), (8, width)],
        partial, swap(partial), pack, other, code, m4_in,
    )
    p1_in, p2_in = move(first, 1, -1), move(second, 2, -2)
    p3_in, p4_in, fifth_in = (move(rhs, j, -j) for j in range(3, 6))
    sixth_in = lax.ppermute(sixth, GRID, [(tiles + t, tiles + (t + 6) % tiles) for t in range(tiles)])
    (near,) = call(near_kernel, [(72, width)], p1_in, p2_in, m1_in, m2_in)
    window = (6 * lines + 16, width)
    send, keep = call(
        trace_kernel, [(2 * lines, width)] * 2,
        pack, other, share, code, rhs, swap(near), fifth_in, sixth_in, p1_in, p2_in, p3_in, p4_in, *messages_in,
        scratch=[pltpu.VMEM(window, F32)] * 5
        + [pltpu.VMEM((window[0], width // 2), F32)] * 2,
    )
    both = keep + swap(send)
    return (both[:lines] / both[lines:])[None]


def solution(mesh):
    table = P(GRID, None)
    grid = P("comp", "tile", None)
    return jax.shard_map(
        shards,
        mesh=mesh,
        in_specs=(grid, grid, P("tile", None), table, table, table),
        out_specs=grid,
        check_vma=False,
    )
```

```python
import jax
import jax.experimental.pallas as pl
import jax.experimental.pallas.tpu as pltpu
import jax.numpy as jnp
from jax import lax
from jax.sharding import PartitionSpec as P

SPAN = 8
SWEEPS = 20
MIDDLE = SPAN // 2
F32 = jnp.float32
BF16 = jnp.bfloat16
I32 = jnp.int32
CONTRACT_LANES = (((1,), (1,)), ((), ()))
GRID = ("comp", "tile")


def call(kernel, shapes, *operands, scratch=(), where=pltpu.VMEM, flops=None):
    out = [jax.ShapeDtypeStruct(shape, F32) for shape in shapes]
    cost = None
    if flops is not None:
        cost = pl.CostEstimate(flops=flops, bytes_accessed=0, transcendentals=0)
    return pl.pallas_call(
        kernel,
        out_shape=out,
        in_specs=[pl.BlockSpec(memory_space=where)] * len(operands),
        out_specs=[pl.BlockSpec(memory_space=pltpu.VMEM)] * len(out),
        scratch_shapes=scratch,
        cost_estimate=cost,
        compiler_params=pltpu.CompilerParams(vmem_limit_bytes=32 * 1024 * 1024),
    )(*operands)


def on_each_component(atmosphere, ocean):
    comp = lax.axis_index("comp")
    pl.when(comp == 0)(atmosphere)
    pl.when(comp != 0)(ocean)


def fold(source, target, first, halves):
    width = halves.shape[1]
    rows = halves.shape[0]
    lines = rows // SPAN
    for h in range(target.shape[1] // width):
        for j in range(lines):
            at = j * target.shape[1] + h * width
            halves[pl.ds(j, SPAN, stride=lines), :] = source[:, at : at + width].astype(F32)
        target[first : first + rows, h * width : h * width + width] = halves[...]


def gather_steps(table, index, out):
    rows, width = index.shape
    tiles = [(r, h) for r in range(0, rows, 8) for h in range(0, width, 128)]
    pieces = [index[r : r + 8, h : h + 128] for r, h in tiles]
    high = [lax.shift_right_logical(p, 7) for p in pieces]
    low = [p & 127 for p in pieces]
    found = [jnp.zeros((8, 128), F32) for _ in tiles]
    for i in range(rows * width // 128):
        r, h = divmod(i * 128, width)
        line = jnp.broadcast_to(table[r : r + 1, h : h + 128], (8, 128))
        for k in range(len(tiles)):
            picked = jnp.take_along_axis(line, low[k], axis=1, mode="promise_in_bounds")
            found[k] = jnp.where(high[k] == i, picked, found[k])
        yield
    across = width // 128
    lines = [jnp.concatenate(found[k : k + across], 1) for k in range(0, len(found), across)]
    out.append(jnp.concatenate(lines, 0))


def scatter_steps(totals, values, index):
    rows, width = index.shape
    place = lax.broadcasted_iota(I32, (64, width), 0)
    for r in range(rows):
        cell = index[r : r + 1, :]
        value = values[r : r + 1, :]
        head = value.astype(BF16).astype(F32)
        tail = value - head
        row_here = place == lax.shift_right_logical(cell, 6)
        column_here = place == (cell & 63)
        spread = jnp.concatenate(
            [
                jnp.where(row_here, head, 0.0).astype(BF16),
                jnp.where(row_here, tail, 0.0).astype(BF16),
            ],
            0,
        )
        chosen = jnp.where(column_here, 1.0, 0.0).astype(BF16)
        totals.append(
            totals.pop()
            + lax.dot_general(spread, chosen, CONTRACT_LANES, preferred_element_type=F32)
        )
        yield


def remap(parts, total):
    totals = [total]
    adding = iter(())
    for table, cells, weights, targets in parts:
        found = []
        for step, _ in enumerate(gather_steps(table, cells, found)):
            if step % 2:
                next(adding, None)
        for _ in adding:
            pass
        adding = scatter_steps(totals, weights * found[0], targets)
    for _ in adding:
        pass
    return totals[0]


def scatter_add(total, values, index):
    totals = [total]
    for _ in scatter_steps(totals, values, index):
        pass
    return totals[0]


def as_rows(total):
    both = total[:64] + total[64:]
    cells = both.reshape(16, 4, 64)
    return jnp.concatenate([cells[:, q, :] for q in range(4)], 1)


def pack_kernel(cells, weights, slots, state, coeff, vertical, pack, code, ints, reals, codes, halves, sems):
    copies = [
        pltpu.make_async_copy(state.at[0], pack.at[256:272], sems.at[0]),
        pltpu.make_async_copy(coeff.at[0], pack.at[272:288], sems.at[1]),
        pltpu.make_async_copy(vertical, codes, sems.at[2]),
    ]
    for copy in copies:
        copy.start()

    def atmosphere():
        first = pltpu.make_async_copy(cells, ints, sems.at[3])
        second = pltpu.make_async_copy(weights, reals, sems.at[4])
        first.start()
        second.start()
        first.wait()
        fold(ints, pack, 0, halves)
        second.wait()
        fold(reals, pack, 128, halves)

    def ocean():
        first = pltpu.make_async_copy(slots, ints, sems.at[3])
        first.start()
        pack[128:256, :] = jnp.zeros((128, pack.shape[1]), F32)
        first.wait()
        ints[...] = renumbered(ints[...])
        fold(ints, pack, 0, halves)

    on_each_component(atmosphere, ocean)
    for copy in copies:
        copy.wait()
    code[...] = halved(codes[...].astype(F32))

    @pl.when(lax.axis_index("comp") != 0)
    def _():
        pack[256:272, :] = halved(pack[256:272, :])
        pack[272:288, :] = halved(pack[272:288, :])


def halved(x):
    width = x.shape[1] // 2
    a, b = x[:, :width], x[:, width:]
    lane = lax.broadcasted_iota(I32, a.shape, 1)

    def picked(odd):
        index = ((2 * lane) & (width - 1)) + odd
        first = jnp.take_along_axis(a, index, axis=1, mode="promise_in_bounds")
        second = jnp.take_along_axis(b, index, axis=1, mode="promise_in_bounds")
        return jnp.where(lane < width // 2, first, second)

    return jnp.concatenate([picked(0), picked(1)], 1)


def unhalved(a, b):
    lane = lax.broadcasted_iota(I32, a.shape, 1)
    width = a.shape[1]

    def picked(first):
        index = lax.shift_right_logical(lane, 1) + first
        even = jnp.take_along_axis(a, index, axis=1, mode="promise_in_bounds")
        odd = jnp.take_along_axis(b, index, axis=1, mode="promise_in_bounds")
        return jnp.where((lane & 1) == 0, even, odd)

    return jnp.concatenate([picked(0), picked(width // 2)], 1)


def renumbered(cell):
    return (cell & ~255) + lax.shift_left(cell & 1, 7) + lax.shift_right_logical(cell & 255, 1)


def block_of(ref, k):
    return ref[16 * k : 16 * k + 16]


def message_kernel(pack, other, code, m1, m2, m3, m4, edge):
    def fill(air, sea, rows, rows_back):
        s = air[256:272, :]
        coeff = air[272:288, :]
        none = jnp.zeros_like(s[0:1])
        near = jnp.concatenate([none, s[:-1]], 0) + jnp.concatenate([s[1:], none], 0)
        near = near + pltpu.roll(s, 1, 1) + pltpu.roll(s, s.shape[1] - 1, 1)
        flux = coeff * (s + 0.2 * (near - 4.0 * s))
        ends = jnp.concatenate([coeff[0:1], coeff[15:16], s[0:1], s[15:16], none, none, none, none], 0)
        for j, m in enumerate((m1, m2, m3)):
            m[0:16, :] = block_of(air, rows[j])
            m[16:32, :] = block_of(air, 8 + rows[j])
            m[32:48, :] = flux
            m[48:64, :] = block_of(sea, rows_back[j])
            m[64:72, :] = ends
            m[72:88, :] = sea[272:288, :]
            m[88:104, :] = code[...]
            m[104:120, :] = sea[256:272, :]
        m4[32:48, :] = flux
        m4[48:56, :] = ends
        m4[56:72, :] = sea[272:288, :]
        m4[72:88, :] = code[...]
        edge[...] = s[0:8]

    def atmosphere():
        fill(pack, other, (3, 2, 1), (5, 6, 7))
        m4[0:16, :] = block_of(pack, 0)
        m4[16:32, :] = block_of(pack, 8)

    def ocean():
        fill(other, pack, (5, 6, 7), (3, 2, 1))
        m4[0:16, :] = block_of(pack, 0)
        m4[16:32, :] = pack[256:272, :]

    on_each_component(atmosphere, ocean)


def share_kernel(pack, other, share):
    def fill(air, first):
        total = jnp.zeros((128, 64), F32)
        for d in range(first, first + SPAN // 2):
            total = scatter_add(total, block_of(air, 8 + d), block_of(air, d).astype(I32))
        share[...] = as_rows(total)

    on_each_component(lambda: fill(pack, 4), lambda: fill(other, 0))


def edge_kernel(edge, total, out, same):
    out[...] = edge[...]
    same[...] = total[...]


def whole_flux(flux, ends, before, after):
    first = flux[0:1] + ends[0:1] * (0.2 * before)
    last = flux[15:16] + ends[1:2] * (0.2 * after)
    return jnp.concatenate([first, flux[1:15], last], 0)


def flux_part(cells, weights, flux, ends, before, after, slots):
    return whole_flux(flux, ends, before, after), cells.astype(I32), weights, slots.astype(I32)


def sent(m):
    return m[0:16, :], m[16:32, :], m[32:48, :], m[64:72, :]


def first_flux_kernel(m1, m2, m3, pack, other, total):
    atmosphere = lax.axis_index("comp") == 0

    def either(a, b):
        return jnp.where(atmosphere, a, b)

    parts = []
    before = either(pack[271:272, :], m2[67:68, :])
    after = either(m2[66:67, :], other[256:257, :])
    parts.append(flux_part(*sent(m1), before, after, either(block_of(other, 3), block_of(pack, 5))))
    before = either(m1[67:68, :], m3[67:68, :])
    after = either(m3[66:67, :], m1[66:67, :])
    parts.append(flux_part(*sent(m2), before, after, either(block_of(other, 2), block_of(pack, 6))))
    total[...] = remap(parts, jnp.zeros((128, 64), F32))


def second_flux_kernel(edge, m4, m1, m2, m3, own, pack, other, total, partial):
    atmosphere = lax.axis_index("comp") == 0

    def either(a, b):
        return jnp.where(atmosphere, a, b)

    parts = []
    before = either(m3[67:68, :], m1[67:68, :])
    cells = either(m4[0:16, :], block_of(other, 4))
    weights = either(m4[16:32, :], block_of(other, 12))
    flux = either(m4[32:48, :], own[32:48, :])
    ends = either(m4[48:56, :], own[64:72, :])
    slots = either(block_of(other, 0), block_of(pack, 4))
    parts.append(flux_part(cells, weights, flux, ends, before, edge[0:1, :], slots))
    before = either(m2[67:68, :], m4[51:52, :])
    after = either(m4[50:51, :], m2[66:67, :])
    parts.append(flux_part(*sent(m3), before, after, either(block_of(other, 1), block_of(pack, 7))))
    partial[...] = as_rows(remap(parts, total[...]))


def source_kernel(partial, partial_sw, pack, other, code, m4, rhs, first, second, sixth):
    atmosphere = lax.axis_index("comp") == 0
    sea = jnp.where(atmosphere, other[256:272, :], pack[256:272, :])
    total = partial[...] + partial_sw[...] + sea
    rhs[...] = total
    first[0:16, :] = total
    first[16:48, :] = m4[56:88, :]
    second[0:16, :] = total
    second[16:24, :] = m4[64:72, :]
    second[24:32, :] = m4[80:88, :]
    sixth[...] = total[8:16]


def near_kernel(p1, p2, m1, m2, out):
    out[0:16, :] = p1[0:16, :]
    out[16:48, :] = m1[72:104, :]
    out[48:56, :] = p2[8:16, :]
    out[56:64, :] = m2[80:88, :]
    out[64:72, :] = m2[96:104, :]


def trace_kernel(
    pack, other, share, code_own, own, near, fifth, sixth, p1, p2, p3, p4, m1, m2, m3, m4,
    send, keep, rhs, inv, code, code_up, code_down, even, odd,
):
    rows, width = rhs.shape
    groups = rows // 8

    def place(parts):
        at = 0
        for right, diagonal, face in parts:
            size = right.shape[0]
            rhs[at : at + size, :] = right[...]
            inv[at : at + size, :] = 1.0 / (diagonal[...] + 3.0)
            code[at : at + size, :] = face[...]
            at += size

    def thirds(ref, first, step, size):
        return [ref.at[first + k * step : first + k * step + size] for k in range(3)]

    others = [(p.at[0:16], m.at[72:88], m.at[88:104]) for p, m in ((p1, m1), (p2, m2), (p3, m3))]
    others.append((p4, m4.at[56:72], m4.at[72:88]))
    further = p1.at[16:24], p1.at[32:40]
    whole = p1.at[16:32], p1.at[32:48]
    last = p2.at[16:24], p2.at[24:32]
    on_each_component(
        lambda: place(
            [thirds(near, 48, 8, 8), thirds(near, 0, 16, 16), (own, other.at[272:288], code_own), *others,
             (fifth.at[0:8], *further)]
        ),
        lambda: place(
            [(sixth, *last), (fifth, *whole), *others[::-1], (own, pack.at[272:288], code_own),
             thirds(near, 0, 16, 8)]
        ),
    )
    line = lax.broadcasted_iota(I32, (8, width), 0)

    def group(ref, g):
        return ref[8 * g : 8 * g + 8, :]

    def from_above(here, above):
        return jnp.where(line[:, : here.shape[1]] == 0, above, here)

    def from_below(here, below):
        return jnp.where(line[:, : here.shape[1]] == 7, below, here)

    downward = [pltpu.roll(group(code, g), 1, 0) for g in range(groups)]
    for g in range(groups):
        code_down[8 * g : 8 * g + 8, :] = from_above(downward[g], downward[max(g - 1, 0)])
    upward = [pltpu.roll(group(code, g), 7, 0) for g in range(groups)]
    for g in range(groups):
        code_up[8 * g : 8 * g + 8, :] = from_below(upward[g], upward[min(g + 1, groups - 1)])
    half = width // 2
    for g in range(groups):
        first = group(rhs, g) * group(inv, g)
        even[8 * g : 8 * g + 8, :] = first[:, :half]
        odd[8 * g : 8 * g + 8, :] = first[:, half:]

    def sweep(first, last):
        beside, above, below = {}, {}, {}

        def chosen(code, zero, left, here, right):
            return jnp.where(code == zero, left, jnp.where(code == zero + 1.0, here, right))

        def read(g):
            e, o = group(even, g), group(odd, g)
            left = pltpu.roll(o, 1, 1)
            right = pltpu.roll(e, half - 1, 1)
            beside[g] = left + o, e + right
            u, d = group(code_up, g), group(code_down, g)
            up = (chosen(u[:, :half], 0.0, left, e, o), chosen(u[:, half:], 0.0, e, o, right))
            down = (chosen(d[:, :half], 3.0, left, e, o), chosen(d[:, half:], 3.0, e, o, right))
            above[g] = [pltpu.roll(x, 1, 0) for x in up]
            below[g] = [pltpu.roll(x, 7, 0) for x in down]

        def write(g):
            for k, ref in enumerate((even, odd)):
                lanes = slice(k * half, k * half + half)
                up = from_above(above[g][k], above[max(g - 1, first)][k])
                down = from_below(below[g][k], below[min(g + 1, last - 1)][k])
                third = jnp.where(group(code, g)[:, lanes] >= 3.0, down, up)
                total = group(rhs, g)[:, lanes] + (beside[g][k] + third)
                ref[8 * g : 8 * g + 8, :] = total * group(inv, g)[:, lanes]

        for g in range(first, last):
            read(g)
            if g > first:
                write(g - 1)
        write(last - 1)

    def repeat(count, skip):
        for _ in range(count):
            sweep(skip, groups - skip)

    done = 1
    for skip in range(3):
        until = min(SWEEPS, SWEEPS - 16 + 8 * skip)
        repeat(until - done, skip)
        done = until

    atmosphere = lax.axis_index("comp") == 0
    states = [m[104:120, :] for m in (m1, m2, m3)]
    sea = [jnp.where(atmosphere, other[256:272, :], m4[16:32, :])]
    sea += [jnp.where(atmosphere, states[i], states[2 - i]) for i in range(3)]
    slots = [jnp.where(atmosphere, block_of(other, 4), m4[0:16, :])]
    for a, b in ((m1, m3), (m2, m2), (m3, m1)):
        slots.append(jnp.where(atmosphere, a[48:64, :], b[48:64, :]))
    parts = []
    for i in range(4):
        at = 24 + 16 * i
        eta = jnp.concatenate([even[at : at + 16, :], odd[at : at + 16, :]], 1)
        sst = 1.25 * sea[i] + 0.5 * eta - 0.25 * rhs[at : at + 16, :]
        cell = jnp.where(atmosphere, block_of(pack, 4 + i), block_of(other, i)).astype(I32)
        weight = jnp.where(atmosphere, block_of(pack, 12 + i), block_of(other, 8 + i))
        parts.append((sst, slots[i].astype(I32), weight, cell))
    part = as_rows(remap(parts, jnp.zeros((128, 64), F32)))
    send[0:16, :] = jnp.where(atmosphere, unhalved(even[24:40, :], odd[24:40, :]), part)
    send[16:32, :] = jnp.where(atmosphere, 1.0, share[...])
    keep[0:16, :] = jnp.where(atmosphere, part, 0.0)
    keep[16:32, :] = jnp.where(atmosphere, share[...], 0.0)


def shards(state, coeff, vertical, send_cell, incoming_marine_slot, remap_weight):
    tiles = lax.axis_size("tile")
    block = state.shape[1:]
    lines, width = block

    def swap(x):
        return lax.ppermute(x, "comp", [(0, 1), (1, 0)])

    def move(x, atmosphere_from, ocean_from):
        pairs = [((t + atmosphere_from) % tiles, t) for t in range(tiles)]
        pairs += [(tiles + (t + ocean_from) % tiles, tiles + t) for t in range(tiles)]
        return lax.ppermute(x, GRID, pairs)

    arguments = (send_cell, remap_weight, incoming_marine_slot, state, coeff, vertical)
    pack, code = call(
        pack_kernel, [(18 * lines, width), block],
        *[pltpu.with_memory_space_constraint(x, pltpu.HBM) for x in arguments],
        scratch=[
            pltpu.VMEM(send_cell.shape, I32),
            pltpu.VMEM(send_cell.shape, F32),
            pltpu.VMEM(block, I32),
            pltpu.VMEM((SPAN * lines, 128), F32),
            pltpu.SemaphoreType.DMA((5,)),
        ],
        where=pltpu.HBM,
    )
    other = swap(pack)
    tall = 4 * lines + 8
    *messages, edge = call(
        message_kernel,
        [(tall + 3 * lines, width)] * 3 + [(tall + lines, width), (8, width)],
        pack, other, code,
    )
    edge_in = move(edge, 5, 1)
    m1_in, m2_in, m3_in, m4_in = messages_in = [move(m, j, -j) for j, m in enumerate(messages, 1)]
    (share,) = call(share_kernel, [block], pack, other, flops=10**9)
    (total,) = call(first_flux_kernel, [(128, 64)], m1_in, m2_in, m3_in, pack, other, flops=None)
    edge_in, total = call(edge_kernel, [(8, width), (128, 64)], edge_in, total, flops=10**8)
    (partial,) = call(
        second_flux_kernel, [block],
        edge_in, m4_in, m1_in, m2_in, m3_in, messages[1], pack, other, total, flops=10**9,
    )
    rhs, first, second, sixth = call(
        source_kernel,
        [block, (3 * lines, width), (2 * lines, width), (8, width)],
        partial, swap(partial), pack, other, code, m4_in,
    )
    p1_in, p2_in = move(first, 1, -1), move(second, 2, -2)
    p3_in, p4_in, fifth_in = (move(rhs, j, -j) for j in range(3, 6))
    sixth_in = lax.ppermute(sixth, GRID, [(tiles + t, tiles + (t + 6) % tiles) for t in range(tiles)])
    (near,) = call(near_kernel, [(72, width)], p1_in, p2_in, m1_in, m2_in)
    window = (6 * lines + 16, width)
    send, keep = call(
        trace_kernel, [(2 * lines, width)] * 2,
        pack, other, share, code, rhs, swap(near), fifth_in, sixth_in, p1_in, p2_in, p3_in, p4_in, *messages_in,
        scratch=[pltpu.VMEM(window, F32)] * 5
        + [pltpu.VMEM((window[0], width // 2), F32)] * 2,
    )
    both = keep + swap(send)
    return (both[:lines] / both[lines:])[None]


def solution(mesh):
    table = P(GRID, None)
    grid = P("comp", "tile", None)
    return jax.shard_map(
        shards,
        mesh=mesh,
        in_specs=(grid, grid, P("tile", None), table, table, table),
        out_specs=grid,
        check_vma=False,
    )
```
